128 devices in a mesh: grp: 4 (over x_hi, core), tile: 32 (over y, x_lo, z).
Axes of the slice: x: 4 (x_hi: 2, x_lo: 2; x = x_hi * 2 + x_lo), y: 4, z: 4, core: 2. Of those that a mesh axis runs over, the one named last changes fastest.
Arguments:
- soil_head: float32 [8, 1024, 4096], P(None, 'grp', 'tile'), may hold values from -2 to 0.5
- soil_type: int32 [8, 1024, 4096], P(None, 'grp', 'tile'), may hold values from 0 to 11
- soil_table: float32 [3, 12], replicated, may hold values from 0.2 to 2
- emitter_cell: int32 [4, 32, 64], P('grp', 'tile'), may hold values from 0 to 262143
- emitter_rate: float32 [4, 32, 64], P('grp', 'tile'), may hold values from 0.5 to 2
- pond_depth: float32 [1024, 4096], P(('grp', 'tile')), may hold values from 0 to 0.5
- elevation: float32 [1024, 4096], P(('grp', 'tile')), may hold values from 0 to 2
- roughness: float32 [1024, 4096], P(('grp', 'tile')), may hold values from 0.2 to 5
- ponding: int32 [1024, 4096], P(('grp', 'tile')), may hold values 0 or 1
- rain_rate: float32 [1024, 4096], P(('grp', 'tile')), may hold values from 0 to 0.5
Outputs:
- head_next: float32 [8, 1024, 4096], P(None, 'grp', 'tile')
- depth_next: float32 [1024, 4096], P(('grp', 'tile'))
The draws below stay inside these ranges and needn't reach their ends.
Inputs may be any that keep to these rules, and one draw needn't show every extreme that they name: `emitter_cell`: each entry is layer * 256 * 128 + row * 128 + column of a cell in the owning device's block.
All inputs are finite; a program needn't handle non-finite values. No bound on the sum of `ponding` on one device may be relied on, other than what follows from the above.
Results may differ from the reference program's by a relative error of at most 0.00002.
Values sent between devices are 32-bit elements; how exact they have to be, the bound alone decides.
A program may use at most 128 MiB of HBM per device.

```python
import math
import jax
import jax.numpy as jnp
from jax import lax

NZ = 8
SX = 256
SY = 128
NTYPES = 12
EMIT = 64
STEPS = 2
PICARD = 2
SUB_SWEEPS = 2
SURF_SWEEPS = 2
NX = 1024
NY = 4096
N_GRP = 4
N_TILE = 32


def set_ends(array, key, smallest, high):
    longest = array.shape.index(max(array.shape))
    spots = []
    for shift in (0, 1):
        where = [jax.random.randint(jax.random.fold_in(key, axis), (), 0, length) for axis, length in enumerate(array.shape)]
        where[longest] = (where[longest] + shift) % array.shape[longest]
        spots.append(tuple(where))
    return array.at[spots[0]].set(smallest).at[spots[1]].set(high)


def block_levels(rng, shape, split, least, largest):
    factor_of, own = 1.0, jax.random.fold_in(rng, 6)
    for dim, shards_of in split:
        draws = jnp.exp(jax.random.uniform(jax.random.fold_in(own, dim), (shards_of,), jnp.float32, least / len(split), largest / len(split)))
        factor_of = factor_of * jnp.repeat(draws, shape[dim] // shards_of).reshape([-1 if axis == dim else 1 for axis in range(len(shape))])
    return factor_of


def setup_inputs(seed: int = 0) -> dict:
    arg_keys = jax.random.split(jax.random.key(seed), 11)
    return {
        "soil_head": jnp.clip(-2.0 + 2.5 * jax.random.uniform(arg_keys[0], (NZ, NX, NY), jnp.float32) ** block_levels(arg_keys[0], (NZ, NX, NY), ((1, 4), (2, 32)), -0.2, 0.2), -2.0, 0.5),
        "soil_type": set_ends(jax.random.randint(arg_keys[1], (NZ, NX, NY), 0, NTYPES), jax.random.fold_in(arg_keys[1], 1), 0, NTYPES - 1).astype(jnp.int32),
        "soil_table": jnp.clip(jnp.exp(jax.random.uniform(arg_keys[2], (3, NTYPES), jnp.float32, math.log(0.2), math.log(2.0))), 0.2, 2.0),
        "emitter_cell": set_ends(jax.random.randint(arg_keys[3], (N_GRP, N_TILE, EMIT), 0, NZ * SX * SY), jax.random.fold_in(arg_keys[3], 1), 0, (NZ * SX * SY) - 1).astype(jnp.int32),
        "emitter_rate": jnp.clip(0.5 + 1.5 * jax.random.uniform(arg_keys[4], (N_GRP, N_TILE, EMIT), jnp.float32) ** block_levels(arg_keys[4], (N_GRP, N_TILE, EMIT), ((0, 4), (1, 32)), -0.2, 0.2), 0.5, 2.0),
        "pond_depth": jnp.clip(0.5 * jax.random.uniform(arg_keys[5], (NX, NY), jnp.float32) ** block_levels(arg_keys[5], (NX, NY), ((0, 128),), -0.2, 0.2), 0.0, 0.5),
        "elevation": jnp.clip(2.0 * jax.random.uniform(arg_keys[6], (NX, NY), jnp.float32) ** block_levels(arg_keys[6], (NX, NY), ((0, 128),), -0.2, 0.2), 0.0, 2.0),
        "roughness": jnp.clip(jnp.exp(math.log(5.0) - 3.218876 * jax.random.uniform(arg_keys[7], (NX, NY), jnp.float32) ** block_levels(arg_keys[7], (NX, NY), ((0, 128),), -0.2, 0.2)), 0.2, 5.0),
        "ponding": set_ends((jax.random.randint(arg_keys[8], (NX, NY), 0, 5) < 3).astype(jnp.int32), jax.random.fold_in(arg_keys[8], 1), 0, 1),
        "rain_rate": jnp.clip(0.5 * jax.random.uniform(arg_keys[9], (NX, NY), jnp.float32) ** block_levels(arg_keys[9], (NX, NY), ((0, 128),), -0.2, 0.2), 0.0, 0.5),
    }


storage_term = 0.05
film_floor = 0.04
blend_term = 0.05

def lookup(soil_type, soil_table):
    saturated = jnp.zeros(soil_type.shape, jnp.float32)
    shape_rate = jnp.zeros(soil_type.shape, jnp.float32)
    capacity = jnp.zeros(soil_type.shape, jnp.float32)
    for soil_class in range(soil_table.shape[1]):
        matches = soil_type == soil_class
        saturated = jnp.where(matches, soil_table[0, soil_class], saturated)
        shape_rate = jnp.where(matches, soil_table[1, soil_class], shape_rate)
        capacity = jnp.where(matches, soil_table[2, soil_class], capacity)
    return (saturated, shape_rate, capacity)

def conductivity(head_field, saturated, shape_rate):
    return saturated * jnp.exp(shape_rate * jnp.minimum(head_field, 0.0))

def capacity_of(head_field, capacity, shape_rate):
    return capacity * jnp.exp(shape_rate * jnp.minimum(head_field, 0.0)) + storage_term

def six_views(padded):
    return [padded[2:, 1:-1, 1:-1], padded[:-2, 1:-1, 1:-1], padded[1:-1, 2:, 1:-1], padded[1:-1, :-2, 1:-1], padded[1:-1, 1:-1, 2:], padded[1:-1, 1:-1, :-2]]

def four_views(padded):
    return [padded[2:, 1:-1], padded[:-2, 1:-1], padded[1:-1, 2:], padded[1:-1, :-2]]

def soil_sweep(head_pad, cond_pad, conduct, storage, soil_base):
    numerator = soil_base
    denominator = storage
    faces = []
    for side_head, side_cond in zip(six_views(head_pad), six_views(cond_pad)):
        face = 2.0 * conduct * side_cond / (conduct + side_cond)
        faces.append(face)
        numerator = numerator + face * side_head
        denominator = denominator + face
    numerator = numerator + faces[0] - faces[1]
    return numerator / denominator

def surface_sweep(eta_pad, film_pad, film_cond, surface_level, surface_base, top_cond):
    numerator = surface_base
    denominator = 1.0 + top_cond
    for side_eta, side_film in zip(four_views(eta_pad), four_views(film_pad)):
        face = 2.0 * film_cond * side_film / (film_cond + side_film + blend_term)
        numerator = numerator + face * (side_eta - surface_level)
        denominator = denominator + face
    return numerator / denominator

def drip_source(emitter_cell, emitter_rate):
    group_ids = lax.broadcasted_iota(jnp.int32, emitter_cell.shape, 0)
    tile_ids = lax.broadcasted_iota(jnp.int32, emitter_cell.shape, 1)
    cell_layer = emitter_cell // (SX * SY)
    cell_rest = emitter_cell % (SX * SY)
    cell_row = cell_rest // SY
    cell_column = cell_rest % SY
    flat_index = (cell_layer * NX + group_ids * SX + cell_row) * NY + tile_ids * SY + cell_column
    source = jnp.zeros((NZ * NX * NY,), jnp.float32)
    source = source.at[flat_index.reshape(-1).astype(jnp.int32)].add(emitter_rate.reshape(-1))
    return source.reshape(NZ, NX, NY)

def reference(soil_head, soil_type, soil_table, emitter_cell, emitter_rate, pond_depth, elevation, roughness, ponding, rain_rate):
    saturated, shape_rate, capacity = lookup(soil_type, soil_table)
    emitted = drip_source(emitter_cell, emitter_rate)
    film_gain = roughness * ponding.astype(jnp.float32)
    head_step, depth_step = (soil_head, pond_depth)
    for step_index in range(STEPS):
        head_iter, depth_iter = (head_step, depth_step)
        for picard_index in range(PICARD):
            conduct = conductivity(head_iter, saturated, shape_rate)
            storage = capacity_of(head_iter, capacity, shape_rate)
            top_head = head_iter[-1]
            top_cond = conduct[-1]
            film_cond = film_gain * jnp.sqrt(depth_iter * depth_iter + film_floor)
            film_pad = jnp.pad(film_cond, 1)
            surface_base = depth_step + rain_rate + top_cond * top_head
            depth_new = depth_iter
            for sweep_index in range(SURF_SWEEPS):
                eta_pad = jnp.pad(elevation + depth_new, 1)
                depth_new = surface_sweep(eta_pad, film_pad, film_cond, elevation, surface_base, top_cond)
            infiltration = top_cond * (depth_new - top_head)
            soil_base = (storage * head_step + emitted).at[-1].add(infiltration)
            cond_pad = jnp.pad(conduct, 1)
            head_new = head_iter
            for sweep_index in range(SUB_SWEEPS):
                head_new = soil_sweep(jnp.pad(head_new, 1), cond_pad, conduct, storage, soil_base)
            head_iter, depth_iter = (head_new, depth_new)
        head_step, depth_step = (head_iter, depth_iter)
    return (head_step, depth_step)
```

```python
import jax
import jax.numpy as jnp
from jax import lax
from jax.experimental import pallas as pl
from jax.experimental.pallas import tpu as pltpu
from jax.sharding import PartitionSpec as P

MESH = pl.DeviceIdType.MESH
STEPS = 2
PICARD = 2
ROUNDS = STEPS * PICARD
CHUNK = 32
LANES = 128
PAD = 8
STORAGE = 0.05
FILM_FLOOR = 0.04
BLEND = 0.05
LOG2E = 1.4426950408889634
LEFT, RIGHT, UP, DOWN = 0, 1, 2, 3


def inverse(x):
    r = pl.reciprocal(x, approx=True)
    return r * (2.0 - x * r)


def face_of(a, b):
    return (a + a) * b * inverse(a + b)


def film_face(a, b):
    return (a + a) * b * inverse(a + b + BLEND)


def conduct_of(head, saturated, rate):
    return saturated * jnp.exp2(rate * jnp.minimum(head, 0.0))


def to_right(x):
    return pltpu.roll(x, 1, 1)


def to_left(x):
    return pltpu.roll(x, LANES - 1, 1)


def make_kernel(n_grp, n_tile, layers, rows, n_types, n_emit):
    blocks = rows // 8
    groups = layers // 2
    top = layers - 1
    chunk = min(CHUNK, rows)
    starts = range(0, rows, chunk)

    def kernel(
        head_in, type_in, table, cell, rate, depth_in, elev_in, rough_in, pond_in, rain_in,
        head_out, depth_out,
        HH, G1, K, FX, FY, FZ, RD, B, C, SAT, SHP, CAP, EM, TYPE,
        A_SEND, A_RECV, ROUGH, POND, D, ETA, ETA2, FILM, GX, GY, SB, SRD,
        PK, FE, FH, PKS, FEC, STAT_HALO,
        SC, RC, SR, RR, SSC, SRC, SSR, SRR,
        TC, TRC, TR, TRR, SGE, ROWF,
        load_sem, a_send, a_recv, o_send, o_recv, out_sem,
        c_send, c_recv, s_send, s_recv, t_send, t_recv,
    ):
        g = lax.axis_index("grp")
        t = lax.axis_index("tile")
        has = (t > 0, t < n_tile - 1, g > 0, g < n_grp - 1)
        came = (t < n_tile - 1, t > 0, g < n_grp - 1, g > 0)
        target = ((g, t - 1), (g, t + 1), (g - 1, t), (g + 1, t))

        loads = [
            pltpu.make_async_copy(rough_in, ROUGH, load_sem.at[0]),
            pltpu.make_async_copy(pond_in, POND, load_sem.at[1]),
            pltpu.make_async_copy(depth_in, A_SEND.at[0], load_sem.at[2]),
            pltpu.make_async_copy(elev_in, A_SEND.at[1], load_sem.at[3]),
            pltpu.make_async_copy(rain_in, A_SEND.at[3], load_sem.at[4]),
            pltpu.make_async_copy(type_in, TYPE, load_sem.at[5]),
            pltpu.make_async_copy(
                head_in, HH.at[0, pl.ds(1, layers), pl.ds(PAD, rows)], load_sem.at[6]
            ),
        ]
        for copy in loads:
            copy.start()

        barrier = pltpu.get_barrier_semaphore()

        @pl.loop(1, n_tile)
        def _(d):
            pl.semaphore_signal(
                barrier, inc=1, device_id=(g, lax.rem(t + d, n_tile)), device_id_type=MESH
            )

        for side in (UP, DOWN):

            @pl.when(has[side])
            def _():
                pl.semaphore_signal(barrier, inc=1, device_id=target[side], device_id_type=MESH)

        lane = lax.broadcasted_iota(jnp.int32, (8, LANES), 1)
        even = lax.rem(lane, 2) == 0
        low_half = lane < LANES // 2
        ends = (lane == 0) | (lane == LANES - 1)
        inner = jnp.where(
            lax.broadcasted_iota(jnp.int32, (chunk, LANES), 1) == LANES - 1, 0.0, 1.0
        ).astype(jnp.float32)
        zero8 = jnp.zeros((8, LANES), jnp.float32)

        full = rows + 2 * PAD
        plane = jnp.zeros((full, LANES), jnp.float32)
        for ref in (HH.at[0], HH.at[1], G1, K):
            ref[0, :, :] = plane
            ref[layers + 1, :, :] = plane

        @pl.loop(0, layers)
        def _(z):
            for ref in (HH.at[0], HH.at[1], G1, K):
                ref[z + 1, pl.ds(0, PAD), :] = zero8
                ref[z + 1, pl.ds(PAD + rows, PAD), :] = zero8
            FX[z, pl.ds(0, PAD), :] = zero8

        FZ[0, :, :] = jnp.zeros((rows, LANES), jnp.float32)
        for ref in (ETA, ETA2, FILM, GX):
            ref[pl.ds(0, PAD), :] = zero8
            ref[pl.ds(PAD + rows, PAD), :] = zero8

        for side in range(4):

            @pl.when(jnp.logical_not(came[side]))
            def _():
                @pl.loop(0, 2 * ROUNDS)
                def _(e):
                    if side < 2:
                        RC[e, side] = jnp.zeros((groups, 8, LANES), jnp.float32)
                        TRC[e, side] = jnp.zeros((2, 8, LANES), jnp.float32)
                    else:
                        RR[e, side - 2] = zero8
                        TRR[e, side - 2] = zero8

                if side < 2:
                    SRC[side] = jnp.zeros((2, groups, 8, LANES), jnp.float32)
                else:
                    SRR[side - 2] = jnp.zeros((2, 8, LANES), jnp.float32)

        for copy in loads[:5]:
            copy.wait()
        A_SEND[2] = ROUGH[...] * POND[...].astype(jnp.float32)
        own = pltpu.make_async_copy(
            A_SEND.at[:, :, pl.ds(pl.multiple_of(t * LANES, LANES), LANES)],
            A_RECV.at[:, pl.ds(pl.multiple_of(t * 8, 8), 8), :],
            a_recv,
        )
        own.start()

        beside = came[UP].astype(jnp.int32) + came[DOWN].astype(jnp.int32)
        pl.semaphore_wait(barrier, n_tile - 1 + beside)

        @pl.loop(1, n_tile)
        def _(d):
            peer = lax.rem(t + d, n_tile)
            pltpu.make_async_remote_copy(
                src_ref=A_SEND.at[:, :, pl.ds(pl.multiple_of(peer * LANES, LANES), LANES)],
                dst_ref=A_RECV.at[:, pl.ds(pl.multiple_of(t * 8, 8), 8), :],
                send_sem=a_send,
                recv_sem=a_recv,
                device_id=(g, peer),
                device_id_type=MESH,
            ).start()

        def side_copies(cols, cols_recv, rws, rws_recv, send, recv):
            copies = []
            for side in range(4):
                src = cols if side < 2 else rws.at[side - 2]
                dst = cols_recv.at[side] if side < 2 else rws_recv.at[side - 2]
                copies.append(
                    pltpu.make_async_remote_copy(
                        src_ref=src,
                        dst_ref=dst,
                        send_sem=send.at[side],
                        recv_sem=recv.at[side],
                        device_id=target[side],
                        device_id_type=MESH,
                    )
                )
            return copies

        def soil_copies(e):
            return side_copies(SC.at[e], RC.at[e], SR.at[e], RR.at[e], c_send.at[e], c_recv.at[e])

        def surface_copies(e):
            return side_copies(TC.at[e], TRC.at[e], TR.at[e], TRR.at[e], t_send.at[e], t_recv.at[e])

        def static_copies():
            return side_copies(SSC, SRC, SSR, SRR, s_send, s_recv)

        def start(copies):
            for side in range(4):

                @pl.when(has[side])
                def _():
                    copies[side].start()

        def wait_recv(copies):
            for side in range(4):

                @pl.when(came[side])
                def _():
                    copies[side].wait_recv()

        def wait_send(copies):
            for side in range(4):

                @pl.when(has[side])
                def _():
                    copies[side].wait_send()

        def pack(value, first, packed):
            for i in range(value.shape[0] // 8):
                k = first // 8 + i
                moved = pltpu.roll(value[8 * i : 8 * i + 8], (2 * k + 1) % LANES, 1)
                packed = jnp.where(lax.div(lane, 2) == k, moved, packed)
            return packed

        def unpack(packed, first, count):
            parts = []
            for i in range(count // 8):
                k = first // 8 + i
                moved = pltpu.roll(packed, (-(2 * k + 1)) % LANES, 1)
                parts.append(jnp.where(ends, moved, 0.0))
            return jnp.concatenate(parts, axis=0) if len(parts) > 1 else parts[0]

        def compact(src, put):
            for m in range(groups):
                put(m, jnp.where(low_half, src[2 * m], pltpu.roll(src[2 * m + 1], LANES // 2, 1)))

        def expand(dst, m, value):
            dst[2 * m] = value
            dst[2 * m + 1] = pltpu.roll(value, LANES // 2, 1)

        def meet(from_right, from_left):
            return jnp.where(even, to_left(from_right), to_right(from_left))

        loads[5].wait()
        loads[6].wait()

        @pl.loop(0, layers)
        def _(z):
            packs = [zero8, zero8, zero8]
            for r in starts:
                kind = TYPE[z, pl.ds(r, chunk), :]
                sat = jnp.zeros(kind.shape, jnp.float32)
                shp = sat
                cap = sat
                for c in range(n_types):
                    same = kind == c
                    sat = jnp.where(same, table[0, c], sat)
                    shp = jnp.where(same, table[1, c] * LOG2E, shp)
                    cap = jnp.where(same, table[2, c], cap)
                SAT[z, pl.ds(r, chunk), :] = sat
                SHP[z, pl.ds(r, chunk), :] = shp
                CAP[z, pl.ds(r, chunk), :] = cap
                head = HH[0, z + 1, pl.ds(PAD + r, chunk), :]
                for n, value in enumerate((head, sat, shp)):
                    packs[n] = pack(value, r, packs[n])
                if r == 0:
                    SR[0, 0, pl.ds(z, 1), :] = head[:1]
                    SSR[0, 0, pl.ds(z, 1), :] = sat[:1]
                    SSR[0, 1, pl.ds(z, 1), :] = shp[:1]
                if r == starts[-1]:
                    SR[0, 1, pl.ds(z, 1), :] = head[chunk - 1 :]
                    SSR[1, 0, pl.ds(z, 1), :] = sat[chunk - 1 :]
                    SSR[1, 1, pl.ds(z, 1), :] = shp[chunk - 1 :]
            PK[z] = packs[0]
            PKS[0, z] = packs[1]
            PKS[1, z] = packs[2]

        def put_first(m, value):
            SC[0, m] = value

        compact(PK, put_first)
        for n in range(2):

            def put_static(m, value, n=n):
                SSC[n, m] = value

            compact(PKS.at[n], put_static)
        start(soil_copies(0))
        start(static_copies())

        ids = jnp.broadcast_to(cell[0], (LANES, n_emit))
        amount = jnp.broadcast_to(rate[0], (LANES, n_emit))
        cell_row = lax.shift_right_logical(ids, 7)
        column = lax.bitwise_and(ids, LANES - 1)
        here = column == lax.broadcasted_iota(jnp.int32, (LANES, n_emit), 0)
        picked = jnp.where(here, amount, 0.0)
        part0 = picked.astype(jnp.bfloat16)
        rest = picked - part0.astype(jnp.float32)
        part1 = rest.astype(jnp.bfloat16)
        part2 = (rest - part1.astype(jnp.float32)).astype(jnp.bfloat16)

        @pl.loop(0, layers)
        def _(z):
            for r in range(0, rows, min(LANES, rows)):
                size = min(LANES, rows)
                wanted = lax.broadcasted_iota(jnp.int32, (size, n_emit), 0) + (z * rows + r)
                hot = jnp.where(cell_row[:size] == wanted, 1.0, 0.0).astype(jnp.bfloat16)
                total = jnp.zeros((size, LANES), jnp.float32)
                for part in (part2, part1, part0):
                    total = total + lax.dot_general(
                        hot, part, (((1,), (1,)), ((), ())), preferred_element_type=jnp.float32
                    )
                EM[z, pl.ds(r, size), :] = total

        def finish_surface(slot, e):
            packs = [zero8, zero8]
            for r in starts:
                depth = D[slot, pl.ds(r, chunk), :]
                square = depth * depth + FILM_FLOOR
                film = A_RECV[2, pl.ds(r, chunk), :] * (square * lax.rsqrt(square))
                eta = A_RECV[1, pl.ds(r, chunk), :] + depth
                FILM[pl.ds(PAD + r, chunk), :] = film
                ETA[pl.ds(PAD + r, chunk), :] = eta
                packs[0] = pack(eta, r, packs[0])
                packs[1] = pack(film, r, packs[1])
                if r == 0:
                    TR[e, 0, pl.ds(0, 1), :] = eta[:1]
                    TR[e, 0, pl.ds(1, 1), :] = film[:1]
                if r == starts[-1]:
                    TR[e, 1, pl.ds(0, 1), :] = eta[chunk - 1 :]
                    TR[e, 1, pl.ds(1, 1), :] = film[chunk - 1 :]
            TC[e, 0] = packs[0]
            TC[e, 1] = packs[1]
            start(surface_copies(e))

        TR[...] = jnp.zeros(TR.shape, jnp.float32)

        @pl.loop(0, 2 * ROUNDS)
        def _(e):
            TC[e] = jnp.zeros((2, 8, LANES), jnp.float32)

        def surface_sweep(src, r, edge):
            return (
                SB[pl.ds(r, chunk), :]
                + GX[pl.ds(PAD + r, chunk), :] * src[pl.ds(PAD + r + 1, chunk), :]
                + GX[pl.ds(PAD + r - 1, chunk), :] * src[pl.ds(PAD + r - 1, chunk), :]
                + GY[pl.ds(r, chunk), :] * to_left(src[pl.ds(PAD + r, chunk), :])
                + to_right(GY[pl.ds(r, chunk), :] * src[pl.ds(PAD + r, chunk), :])
                + unpack(edge, r, chunk)
            ) * SRD[pl.ds(r, chunk), :]

        def soil_numerator(src, z, r, base, fx, fxm, fy, fz, fzm, edge):
            here = src[z + 1, pl.ds(PAD + r, chunk), :]
            return (
                base
                + fx * src[z + 1, pl.ds(PAD + r + 1, chunk), :]
                + fxm * src[z + 1, pl.ds(PAD + r - 1, chunk), :]
                + fy * to_left(here)
                + to_right(fy * here)
                + fz * src[z + 2, pl.ds(PAD + r, chunk), :]
                + fzm * src[z, pl.ds(PAD + r, chunk), :]
                + unpack(edge, r, chunk)
            )

        def put_soil(value, z, r, dst, e, packed):
            dst[z + 1, pl.ds(PAD + r, chunk), :] = value
            if r == 0:
                SR[e, 0, pl.ds(z, 1), :] = value[:1]
            if r == starts[-1]:
                SR[e, 1, pl.ds(z, 1), :] = value[chunk - 1 :]
            return pack(value, r, packed)

        def first_sweep(src, z, e):
            packed = zero8
            face = FE[z]
            edge = FH[z]
            for r in starts:
                fx = FX[z, pl.ds(PAD + r, chunk), :]
                fxm = FX[z, pl.ds(PAD + r - 1, chunk), :]
                fy = FY[z, pl.ds(r, chunk), :]
                fz = FZ[z + 1, pl.ds(r, chunk), :]
                fzm = FZ[z, pl.ds(r, chunk), :]
                total = C[z, pl.ds(r, chunk), :] + fx + fxm + fy + to_right(fy) + fz + fzm
                scale = inverse(total + unpack(face, r, chunk))
                RD[z, pl.ds(r, chunk), :] = scale
                base = B[z, pl.ds(r, chunk), :] + (fz - fzm)
                B[z, pl.ds(r, chunk), :] = base
                value = soil_numerator(src, z, r, base, fx, fxm, fy, fz, fzm, edge) * scale
                packed = put_soil(value, z, r, G1, e, packed)
            PK[z] = packed

        def second_sweep(dst, z, e):
            packed = zero8
            edge = FH[z]
            for r in starts:
                fx = FX[z, pl.ds(PAD + r, chunk), :]
                fxm = FX[z, pl.ds(PAD + r - 1, chunk), :]
                fy = FY[z, pl.ds(r, chunk), :]
                fz = FZ[z + 1, pl.ds(r, chunk), :]
                fzm = FZ[z, pl.ds(r, chunk), :]
                base = B[z, pl.ds(r, chunk), :]
                value = soil_numerator(G1, z, r, base, fx, fxm, fy, fz, fzm, edge)
                value = value * RD[z, pl.ds(r, chunk), :]
                packed = put_soil(value, z, r, dst, e, packed)
            PK[z] = packed

        def send_soil(e):
            def put(m, value):
                SC[e, m] = value

            compact(PK, put)
            start(soil_copies(e))

        def halo_rows(dst, e):
            for z in range(layers):
                dst[z + 1, pl.ds(PAD - 1, 1), :] = RR[e, 1, pl.ds(z, 1), :]
                dst[z + 1, pl.ds(PAD + rows, 1), :] = RR[e, 0, pl.ds(z, 1), :]

        wait_recv(static_copies())
        for m in range(groups):
            for n in range(2):
                STAT_HALO[n, m] = meet(SRC[0, n, m], SRC[1, n, m])

        @pl.loop(0, ROUNDS)
        def _(p):
            slot = lax.rem(p, 2)
            other = 1 - slot
            e = 2 * p
            src = HH.at[slot]
            dst = HH.at[other]

            @pl.loop(0, layers)
            def _(z):
                for r in starts:
                    grow = jnp.exp2(
                        SHP[z, pl.ds(r, chunk), :]
                        * jnp.minimum(src[z + 1, pl.ds(PAD + r, chunk), :], 0.0)
                    )
                    K[z + 1, pl.ds(PAD + r, chunk), :] = SAT[z, pl.ds(r, chunk), :] * grow
                    store = CAP[z, pl.ds(r, chunk), :] * grow + STORAGE
                    C[z, pl.ds(r, chunk), :] = store
                    B[z, pl.ds(r, chunk), :] = (
                        store * HH[0, z + 1, pl.ds(PAD + r, chunk), :]
                        + EM[z, pl.ds(r, chunk), :]
                    )

            @pl.loop(0, layers)
            def _(z):
                for r in starts:
                    k = K[z + 1, pl.ds(PAD + r, chunk), :]
                    FX[z, pl.ds(PAD + r, chunk), :] = face_of(
                        k, K[z + 1, pl.ds(PAD + r + 1, chunk), :]
                    )
                    FY[z, pl.ds(r, chunk), :] = face_of(k, to_left(k)) * inner
                    FZ[z + 1, pl.ds(r, chunk), :] = face_of(k, K[z + 2, pl.ds(PAD + r, chunk), :])

            wait_recv(soil_copies(e))
            for m in range(groups):
                mine = conduct_of(SC[e, m], SSC[0, m], SSC[1, m])
                halo = meet(RC[e, 0, m], RC[e, 1, m])
                theirs = conduct_of(halo, STAT_HALO[0, m], STAT_HALO[1, m])
                face = face_of(mine, theirs)
                FEC[m] = face
                expand(FE, m, face)
                expand(FH, m, face * halo)
            halo_rows(src, e)
            for side in range(2):
                mine = conduct_of(SR[e, side], SSR[side, 0], SSR[side, 1])
                halo = RR[e, 1 - side]
                theirs = conduct_of(halo, SRR[1 - side, 0], SRR[1 - side, 1])
                ROWF[side] = face_of(mine, theirs)
            for z in range(layers):
                FX[z, pl.ds(PAD - 1, 1), :] = ROWF[0, pl.ds(z, 1), :]
                FX[z, pl.ds(PAD + rows - 1, 1), :] = ROWF[1, pl.ds(z, 1), :]

            @pl.when(p == 0)
            def _():
                pltpu.make_async_copy(A_RECV, A_RECV, a_recv).wait()
                D[0] = A_RECV[0]
                finish_surface(0, 0)

            wait_recv(surface_copies(e))
            FILM[pl.ds(PAD - 1, 1), :] = TRR[e, 1, pl.ds(1, 1), :]
            FILM[pl.ds(PAD + rows, 1), :] = TRR[e, 0, pl.ds(1, 1), :]
            ETA[pl.ds(PAD - 1, 1), :] = TRR[e, 1, pl.ds(0, 1), :]
            ETA[pl.ds(PAD + rows, 1), :] = TRR[e, 0, pl.ds(0, 1), :]
            film_edge = film_face(TC[e, 1], meet(TRC[e, 0, 1], TRC[e, 1, 1]))
            eta_edge = film_edge * meet(TRC[e, 0, 0], TRC[e, 1, 0])
            SGE[...] = film_edge
            GX[pl.ds(PAD - 1, 1), :] = film_face(FILM[pl.ds(PAD - 1, 1), :], FILM[pl.ds(PAD, 1), :])
            for r in starts:
                film = FILM[pl.ds(PAD + r, chunk), :]
                GX[pl.ds(PAD + r, chunk), :] = film_face(
                    film, FILM[pl.ds(PAD + r + 1, chunk), :]
                )
                GY[pl.ds(r, chunk), :] = film_face(film, to_left(film)) * inner
            for r in starts:
                gy = GY[pl.ds(r, chunk), :]
                faces = (
                    GX[pl.ds(PAD + r, chunk), :]
                    + GX[pl.ds(PAD + r - 1, chunk), :]
                    + gy
                    + to_right(gy)
                    + unpack(film_edge, r, chunk)
                )
                cond = K[top + 1, pl.ds(PAD + r, chunk), :]
                base = D[0, pl.ds(r, chunk), :] + A_RECV[3, pl.ds(r, chunk), :]
                base = base + cond * src[top + 1, pl.ds(PAD + r, chunk), :]
                SB[pl.ds(r, chunk), :] = base - faces * A_RECV[1, pl.ds(r, chunk), :]
                SRD[pl.ds(r, chunk), :] = inverse(1.0 + cond + faces)
            packed = zero8
            for r in starts:
                eta = surface_sweep(ETA, r, eta_edge) + A_RECV[1, pl.ds(r, chunk), :]
                ETA2[pl.ds(PAD + r, chunk), :] = eta
                packed = pack(eta, r, packed)
                if r == 0:
                    TR[e + 1, 0, pl.ds(0, 1), :] = eta[:1]
                if r == starts[-1]:
                    TR[e + 1, 1, pl.ds(0, 1), :] = eta[chunk - 1 :]
            TC[e + 1, 0] = packed
            start(surface_copies(e + 1))

            @pl.loop(0, top)
            def _(z):
                first_sweep(src, z, e + 1)

            wait_recv(surface_copies(e + 1))
            ETA2[pl.ds(PAD - 1, 1), :] = TRR[e + 1, 1, pl.ds(0, 1), :]
            ETA2[pl.ds(PAD + rows, 1), :] = TRR[e + 1, 0, pl.ds(0, 1), :]
            eta_edge2 = SGE[...] * meet(TRC[e + 1, 0, 0], TRC[e + 1, 1, 0])
            for r in starts:
                depth = surface_sweep(ETA2, r, eta_edge2)
                D[other, pl.ds(r, chunk), :] = depth
                cond = K[top + 1, pl.ds(PAD + r, chunk), :]
                gap = depth - src[top + 1, pl.ds(PAD + r, chunk), :]
                B[top, pl.ds(r, chunk), :] = B[top, pl.ds(r, chunk), :] + cond * gap

            @pl.when(p < ROUNDS - 1)
            def _():
                finish_surface(other, e + 2)

            @pl.when(p == ROUNDS - 1)
            def _():
                pltpu.make_async_copy(
                    D.at[0, pl.ds(pl.multiple_of(t * 8, 8), 8), :],
                    depth_out.at[:, pl.ds(pl.multiple_of(t * LANES, LANES), LANES)],
                    o_recv,
                ).start()

                @pl.loop(1, n_tile)
                def _(d):
                    peer = lax.rem(t + d, n_tile)
                    pltpu.make_async_remote_copy(
                        src_ref=D.at[0, pl.ds(pl.multiple_of(peer * 8, 8), 8), :],
                        dst_ref=depth_out.at[:, pl.ds(pl.multiple_of(t * LANES, LANES), LANES)],
                        send_sem=o_send,
                        recv_sem=o_recv,
                        device_id=(g, peer),
                        device_id_type=MESH,
                    ).start()

            first_sweep(src, top, e + 1)
            send_soil(e + 1)
            wait_recv(soil_copies(e + 1))
            for m in range(groups):
                expand(FH, m, FEC[m] * meet(RC[e + 1, 0, m], RC[e + 1, 1, m]))
            halo_rows(G1, e + 1)
            nxt = jnp.minimum(e + 2, 2 * ROUNDS)

            @pl.loop(0, layers)
            def _(z):
                second_sweep(dst, z, nxt)

            @pl.when(p < ROUNDS - 1)
            def _():
                send_soil(e + 2)

        out = pltpu.make_async_copy(
            HH.at[0, pl.ds(1, layers), pl.ds(PAD, rows)], head_out, out_sem
        )
        out.start()

        @pl.loop(0, 2 * ROUNDS)
        def _(e):
            wait_send(soil_copies(e))
            wait_send(surface_copies(e))

        wait_send(static_copies())
        sent = A_SEND.at[:, :, pl.ds(0, (n_tile - 1) * LANES)]
        pltpu.make_async_copy(sent, sent, a_send).wait()
        gone = D.at[0, pl.ds(0, (n_tile - 1) * 8), :]
        pltpu.make_async_copy(gone, gone, o_send).wait()
        pltpu.make_async_copy(depth_out, depth_out, o_recv).wait()
        out.wait()

    full = rows + 2 * PAD
    f32 = jnp.float32
    ex = 2 * ROUNDS

    def vmem(*shape, dtype=f32):
        return pltpu.VMEM(shape, dtype)

    wide = n_tile * LANES
    dma = pltpu.SemaphoreType.DMA
    scratch = [
        vmem(2, layers + 2, full, LANES),
        vmem(layers + 2, full, LANES),
        vmem(layers + 2, full, LANES),
        vmem(layers, full, LANES),
        vmem(layers, rows, LANES),
        vmem(layers + 1, rows, LANES),
        vmem(layers, rows, LANES),
        vmem(layers, rows, LANES),
        vmem(layers, rows, LANES),
        vmem(layers, rows, LANES),
        vmem(layers, rows, LANES),
        vmem(layers, rows, LANES),
        vmem(layers, rows, LANES),
        vmem(layers, rows, LANES, dtype=jnp.int32),
        vmem(4, 8, wide),
        vmem(4, rows, LANES),
        vmem(8, wide),
        vmem(8, wide, dtype=jnp.int32),
        vmem(2, rows, LANES),
        vmem(full, LANES),
        vmem(full, LANES),
        vmem(full, LANES),
        vmem(full, LANES),
        vmem(rows, LANES),
        vmem(rows, LANES),
        vmem(rows, LANES),
        vmem(layers, 8, LANES),
        vmem(layers, 8, LANES),
        vmem(layers, 8, LANES),
        vmem(2, layers, 8, LANES),
        vmem(groups, 8, LANES),
        vmem(2, groups, 8, LANES),
        vmem(ex + 1, groups, 8, LANES),
        vmem(ex, 2, groups, 8, LANES),
        vmem(ex + 1, 2, 8, LANES),
        vmem(ex, 2, 8, LANES),
        vmem(2, groups, 8, LANES),
        vmem(2, 2, groups, 8, LANES),
        vmem(2, 2, 8, LANES),
        vmem(2, 2, 8, LANES),
        vmem(ex, 2, 8, LANES),
        vmem(ex, 2, 2, 8, LANES),
        vmem(ex, 2, 8, LANES),
        vmem(ex, 2, 8, LANES),
        vmem(8, LANES),
        vmem(2, 8, LANES),
        dma((7,)), dma(()), dma(()), dma(()), dma(()), dma(()),
        dma((ex, 4)), dma((ex, 4)), dma((4,)), dma((4,)), dma((ex, 4)), dma((ex, 4)),
    ]
    anywhere = pl.BlockSpec(memory_space=pl.ANY)
    in_vmem = pl.BlockSpec(memory_space=pltpu.VMEM)
    return pl.pallas_call(
        kernel,
        out_shape=(
            jax.ShapeDtypeStruct((layers, rows, LANES), f32),
            jax.ShapeDtypeStruct((8, wide), f32),
        ),
        in_specs=[
            anywhere, anywhere, pl.BlockSpec(memory_space=pltpu.SMEM), in_vmem, in_vmem,
            anywhere, anywhere, anywhere, anywhere, anywhere,
        ],
        out_specs=(anywhere, anywhere),
        scratch_shapes=scratch,
        compiler_params=pltpu.CompilerParams(
            collective_id=0, has_side_effects=True, vmem_limit_bytes=48 * 1024 * 1024
        ),
    )


def solution(mesh):
    n_grp, n_tile = mesh.shape["grp"], mesh.shape["tile"]

    def shards(soil_head, soil_type, soil_table, emitter_cell, emitter_rate, *surface):
        layers, rows, _ = soil_head.shape
        run = make_kernel(
            n_grp, n_tile, layers, rows, soil_table.shape[1], emitter_cell.shape[-1]
        )
        return run(soil_head, soil_type, soil_table, emitter_cell, emitter_rate, *surface)

    cells = P(None, "grp", "tile")
    strip = P(("grp", "tile"), None)
    emitters = P("grp", "tile", None)
    return jax.shard_map(
        shards,
        mesh=mesh,
        in_specs=(cells, cells, P(), emitters, emitters, strip, strip, strip, strip, strip),
        out_specs=(cells, strip),
        check_vma=False,
    )
```

```python
import jax
import jax.numpy as jnp
from jax import lax
from jax.experimental import pallas as pl
from jax.experimental.pallas import tpu as pltpu
from jax.sharding import PartitionSpec as P

MESH = pl.DeviceIdType.MESH
STEPS = 2
PICARD = 2
ROUNDS = STEPS * PICARD
LANES = 128
STORAGE = 0.05
FILM_FLOOR = 0.04
BLEND = 0.05
LOG2E = 1.4426950408889634
OUTSIDE = 1e-30
PLANES = 8
WS, WD = 2, 3
H, SAT, SHP, CAP, EM = 0, 2, 3, 4, 5
SIDES = ((0, -1), (0, 1), (-1, 0), (1, 0), (1, 1), (1, -1), (-1, 1), (-1, -1))


def inverse(x):
    r = pl.reciprocal(x, approx=True)
    return r * (2.0 - x * r)


def face_of(a, b):
    return (a + a) * b * inverse(a + b)


def film_face(a, b):
    return (a + a) * b * inverse(a + b + BLEND)


def roll(x, shift):
    return pltpu.roll(x, shift % LANES, 1)


def make_kernel(n_grp, n_tile, layers, rows, n_types, n_emit):
    XI = rows // 8
    RP = XI + 16
    ZP = (PLANES + 2 * WS) * RP
    SP = (PLANES + 2 * WD) * RP
    nq = XI // 8
    top = layers - 1
    N = XI + 8
    yv = (WD * nq + 7) // 8

    def kernel(
        head_in, type_in, table, cell, rate, depth_in, elev_in, rough_in, pond_in, rain_in,
        head_out, depth_out,
        BIG, G1, K, FX, FY, FZ, RD, B, C, NAT, TYPE,
        A_SEND, A_RECV, ROUGH, POND, DN,
        SF, FILM, ETA, ETA2, GX, GY, SB, SRD,
        YS, YR, XS, XR, CS, CR, TYS, TYR, TXS, TXR, TCS, TCR,
        load_sem, a_send, a_recv, o_send, o_recv, out_sem,
        c_send, c_recv, t_send, t_recv,
    ):
        g = lax.axis_index("grp")
        t = lax.axis_index("tile")

        def inside(dg, dt):
            ok = jnp.bool_(True)
            if dg:
                ok = g + dg >= 0 if dg < 0 else g + dg < n_grp
            if dt:
                side = t + dt >= 0 if dt < 0 else t + dt < n_tile
                ok = jnp.logical_and(ok, side) if dg else side
            return ok

        has = [inside(dg, dt) for dg, dt in SIDES]
        came = [inside(-dg, -dt) for dg, dt in SIDES]
        target = [(g + dg, t + dt) for dg, dt in SIDES]

        loads = [
            pltpu.make_async_copy(rough_in, ROUGH, load_sem.at[0]),
            pltpu.make_async_copy(pond_in, POND, load_sem.at[1]),
            pltpu.make_async_copy(depth_in, A_SEND.at[0], load_sem.at[2]),
            pltpu.make_async_copy(elev_in, A_SEND.at[1], load_sem.at[3]),
            pltpu.make_async_copy(rain_in, A_SEND.at[3], load_sem.at[4]),
            pltpu.make_async_copy(type_in, TYPE, load_sem.at[5]),
            pltpu.make_async_copy(head_in, NAT, load_sem.at[6]),
        ]
        for copy in loads:
            copy.start()

        barrier = pltpu.get_barrier_semaphore()

        @pl.loop(1, n_tile)
        def _(d):
            pl.semaphore_signal(
                barrier, inc=1, device_id=(g, lax.rem(t + d, n_tile)), device_id_type=MESH
            )

        for side in range(2, 8):

            @pl.when(has[side])
            def _():
                pl.semaphore_signal(barrier, inc=1, device_id=target[side], device_id_type=MESH)

        lane = lax.broadcasted_iota(jnp.int32, (8, LANES), 1)
        xb = lax.bitwise_and(lane, 7)
        zero8 = jnp.zeros((8, LANES), jnp.float32)

        @pl.loop(0, ZP // 8)
        def _(r):
            for base in (0, (layers + 1) * ZP):
                at = pl.ds(pl.multiple_of(base + r * 8, 8), 8)
                BIG[H, at, :] = zero8
                BIG[H + 1, at, :] = zero8
                G1[at, :] = zero8
                K[at, :] = zero8
            FZ[pl.ds(pl.multiple_of(r * 8, 8), 8), :] = zero8

        for side in range(8):

            @pl.when(jnp.logical_not(came[side]))
            def _():
                for k in range(5 + ROUNDS - 1):
                    fill = zero8 + OUTSIDE if k == 1 else zero8
                    if side < 2:
                        for z in range(layers):
                            YR[side, k, z] = fill
                    elif side < 4:
                        for v in range(4):
                            XR[side - 2, k, v] = fill
                    else:
                        CR[side - 4, k] = fill
                for k in range(4 + ROUNDS - 1):
                    if side < 2:
                        for v in range(yv):
                            TYR[side, k, v] = zero8
                    elif side < 4:
                        TXR[side - 2, k] = zero8
                    else:
                        TCR[side - 4, k] = zero8

        for copy in loads[:5]:
            copy.wait()
        A_SEND[2] = ROUGH[...] * POND[...].astype(jnp.float32)
        own = pltpu.make_async_copy(
            A_SEND.at[:, :, pl.ds(pl.multiple_of(t * LANES, LANES), LANES)],
            A_RECV.at[:, pl.ds(pl.multiple_of(t * 8, 8), 8), :],
            a_recv,
        )
        own.start()

        beside = jnp.int32(0)
        for side in range(2, 8):
            beside = beside + came[side].astype(jnp.int32)
        pl.semaphore_wait(barrier, n_tile - 1 + beside)

        @pl.loop(1, n_tile)
        def _(d):
            peer = lax.rem(t + d, n_tile)
            pltpu.make_async_remote_copy(
                src_ref=A_SEND.at[:, :, pl.ds(pl.multiple_of(peer * LANES, LANES), LANES)],
                dst_ref=A_RECV.at[:, pl.ds(pl.multiple_of(t * 8, 8), 8), :],
                send_sem=a_send,
                recv_sem=a_recv,
                device_id=(g, peer),
                device_id_type=MESH,
            ).start()

        def copies(bufs, k, count, send, recv):
            y_out, y_in, x_out, x_in, c_out, c_in = bufs
            at = pl.ds(k, count)
            out = []
            for side in range(8):
                if side < 2:
                    src, dst = y_out.at[at], y_in.at[side, at]
                elif side < 4:
                    src, dst = x_out.at[at], x_in.at[side - 2, at]
                else:
                    src, dst = c_out.at[side - 4, at], c_in.at[side - 4, at]
                out.append(
                    pltpu.make_async_remote_copy(
                        src_ref=src,
                        dst_ref=dst,
                        send_sem=send.at[side],
                        recv_sem=recv.at[side],
                        device_id=target[side],
                        device_id_type=MESH,
                    )
                )
            return out

        soil_bufs = (YS, YR, XS, XR, CS, CR)
        surface_bufs = (TYS, TYR, TXS, TXR, TCS, TCR)

        def soil_copies(e):
            if isinstance(e, int) and e == 0:
                return copies(soil_bufs, 0, 5, c_send.at[0], c_recv.at[0])
            return copies(soil_bufs, 4 + e, 1, c_send.at[e], c_recv.at[e])

        def surface_copies(e):
            if isinstance(e, int) and e == 0:
                return copies(surface_bufs, 0, 4, t_send.at[0], t_recv.at[0])
            return copies(surface_bufs, 3 + e, 1, t_send.at[e], t_recv.at[e])

        def start(made):
            for side in (1, 0, 4, 5, 6, 7, 2, 3):

                @pl.when(has[side])
                def _():
                    made[side].start()

        def wait_recv(made):
            for side in range(8):

                @pl.when(came[side])
                def _():
                    made[side].wait_recv()

        def wait_send(made):
            for side in range(8):

                @pl.when(has[side])
                def _():
                    made[side].wait_send()

        def fold(v):
            v = list(v)
            for k in (1, 2, 4):
                low = lax.bitwise_and(lane, k) == 0
                for a in range(8):
                    if a & k == 0:
                        p, q = v[a], v[a | k]
                        v[a] = jnp.where(low, p, roll(q, k))
                        v[a | k] = jnp.where(low, roll(p, -k), q)
            return v

        def soil_row(plane, xi):
            return (plane + WS) * RP + 8 + xi

        def film_row(plane, xi):
            return (plane + WD) * RP + 8 + xi

        def columns_out(R, base, row, width, put):
            packed = zero8
            for a in range(1, width + 1):
                for q in range(nq):
                    i = (a - 1) * nq + q
                    high = roll(R[pl.ds(base + row(PLANES - a, 8 * q), 8), :], 8)
                    low = roll(R[pl.ds(base + row(a - 1, 8 * q), 8), :], -8)
                    R[pl.ds(base + row(-a, 8 * q), 8), :] = high
                    R[pl.ds(base + row(PLANES - 1 + a, 8 * q), 8), :] = low
                    both = jnp.where(lane >= LANES // 2, low, high)
                    slot = i % 8
                    moved = roll(both, 16 * slot + 8)
                    packed = jnp.where(lax.shift_right_logical(lane, 4) == slot, moved, packed)
                    if slot == 7 or i == width * nq - 1:
                        put(i // 8, packed)
                        packed = zero8

        def columns_in(R, base, row, width, get):
            for a in range(1, width + 1):
                for q in range(nq):
                    i = (a - 1) * nq + q
                    if i % 8 == 0:
                        from_right, from_left = get(i // 8)
                        met = jnp.where(lax.bitwise_and(lane, 15) < 8, from_right, from_left)
                    u = roll(met, -(16 * (i % 8) + 8))
                    at = pl.ds(base + row(-a, 8 * q), 8)
                    R[at, :] = jnp.where(lane < 8, u, R[at, :])
                    at = pl.ds(base + row(PLANES - 1 + a, 8 * q), 8)
                    R[at, :] = jnp.where(lane >= LANES - 8, u, R[at, :])

        def rows_out(R, base, row, b, slot, packed):
            high = roll(R[pl.ds(base + row(0, XI - b), 8, stride=RP), :], 1)
            low = roll(R[pl.ds(base + row(0, b - 1), 8, stride=RP), :], -1)
            R[pl.ds(base + row(0, -b), 8, stride=RP), :] = high
            R[pl.ds(base + row(0, XI - 1 + b), 8, stride=RP), :] = low
            both = jnp.where(xb == 7, low, high)
            mine = lax.shift_right_logical(xb, 1) == slot
            return jnp.where(mine, roll(both, 2 * slot + 1), packed)

        def rows_meet(from_down, from_up):
            return jnp.where(lax.bitwise_and(lane, 1) == 1, roll(from_up, -8), roll(from_down, 8))

        def rows_in(R, base, row, b, slot, met):
            u = roll(met, -(2 * slot + 1))
            at = pl.ds(base + row(0, -b), 8, stride=RP)
            R[at, :] = jnp.where(xb == 0, u, R[at, :])
            at = pl.ds(base + row(0, XI - 1 + b), 8, stride=RP)
            R[at, :] = jnp.where(xb == 7, u, R[at, :])

        def corner_source(gather, side, a, b):
            plane = PLANES - a if side in (4, 6) else a - 1
            xi = XI - b if side in (4, 5) else b - 1
            return roll(gather(plane, xi), {4: 1, 5: 113, 6: 15, 7: 127}[side])

        def corner_value(gather, side, a, b, diagonal):
            ln = lane[: diagonal.shape[0]]
            x8 = xb[: diagonal.shape[0]]
            first = side in (4, 6)
            plane = -a if first else PLANES - 1 + a
            if side in (4, 5):
                inner = roll(gather(plane, XI - b), 1)
                other = gather(PLANES - a if first else a - 1, -b)
                near = x8 > 0
            else:
                inner = roll(gather(plane, b - 1), -1)
                other = gather(PLANES - a if first else a - 1, XI - 1 + b)
                near = x8 < 7
            other = roll(other, 8 if first else -8)
            known = ln >= 8 if first else ln < LANES - 8
            return jnp.where(near, inner, jnp.where(known, other, diagonal))

        def corner_place(side, a, b):
            return -a if side in (4, 6) else PLANES - 1 + a, -b if side in (4, 5) else XI - 1 + b

        def soil_out(f, k):
            R = BIG.at[f]

            @pl.loop(0, layers)
            def _(z):
                base = pl.multiple_of((z + 1) * ZP, 8)

                def put(v, value):
                    YS[k, z] = value

                columns_out(R, base, soil_row, WS, put)

            packs = [zero8] * 4
            for z in range(layers):
                for b in range(1, WS + 1):
                    v = (b - 1) * 2 + z // 4
                    packs[v] = rows_out(R, (z + 1) * ZP, soil_row, b, z % 4, packs[v])
            for v in range(4):
                XS[k, v] = packs[v]

            def gather(plane, xi):
                return R[pl.ds(ZP + soil_row(plane, xi), layers, stride=ZP), :]

            for side in range(4, 8):
                CS[side - 4, k] = corner_source(gather, side, 1, 1)

        def soil_in(f, k):
            R = BIG.at[f]

            @pl.loop(0, layers)
            def _(z):
                base = pl.multiple_of((z + 1) * ZP, 8)
                columns_in(R, base, soil_row, WS, lambda v: (YR[0, k, z], YR[1, k, z]))

            met = [rows_meet(XR[0, k, v], XR[1, k, v]) for v in range(4)]
            for z in range(layers):
                for b in range(1, WS + 1):
                    rows_in(R, (z + 1) * ZP, soil_row, b, z % 4, met[(b - 1) * 2 + z // 4])

            def gather(plane, xi):
                return R[pl.ds(ZP + soil_row(plane, xi), layers, stride=ZP), :]

            for side in range(4, 8):
                value = corner_value(gather, side, 1, 1, CR[side - 4, k])
                plane, xi = corner_place(side, 1, 1)
                R[pl.ds(ZP + soil_row(plane, xi), layers, stride=ZP), :] = value

        corners = ((1, 1), (1, 2), (2, 1))

        def surface_out(f, k):
            R = SF.at[f]

            def put(v, value):
                TYS[k, v] = value

            columns_out(R, 0, film_row, WD, put)
            packed = zero8
            for b in range(1, WD + 1):
                packed = rows_out(R, 0, film_row, b, b - 1, packed)
            TXS[k] = packed

            def gather(plane, xi):
                return R[pl.ds(film_row(plane, xi), 1), :]

            for side in range(4, 8):
                for n, (a, b) in enumerate(corners):
                    TCS[side - 4, k, pl.ds(n, 1), :] = corner_source(gather, side, a, b)

        def surface_in(f, k):
            R = SF.at[f]
            columns_in(R, 0, film_row, WD, lambda v: (TYR[0, k, v], TYR[1, k, v]))
            met = rows_meet(TXR[0, k], TXR[1, k])
            for b in range(1, WD + 1):
                rows_in(R, 0, film_row, b, b - 1, met)

            def gather(plane, xi):
                return R[pl.ds(film_row(plane, xi), 1), :]

            for side in range(4, 8):
                for n, (a, b) in enumerate(corners):
                    value = corner_value(gather, side, a, b, TCR[side - 4, k, pl.ds(n, 1), :])
                    plane, xi = corner_place(side, a, b)
                    R[pl.ds(film_row(plane, xi), 1), :] = value

        @pl.loop(0, 4 + ROUNDS - 1)
        def _(k):
            for side in range(4):
                TCS[side, k] = zero8

        loads[5].wait()
        loads[6].wait()

        @pl.loop(0, layers)
        def _(z):
            base = (z + 1) * ZP
            for q in range(nq):
                kinds = fold(
                    [TYPE[z, pl.ds(i * XI + 8 * q, 8), :].astype(jnp.float32) for i in range(8)]
                )
                heads = fold([NAT[z, pl.ds(i * XI + 8 * q, 8), :] for i in range(8)])
                for plane in range(PLANES):
                    at = pl.ds(pl.multiple_of(base + soil_row(plane, 8 * q), 8), 8)
                    sat = shp = cap = zero8
                    for c in range(n_types):
                        same = kinds[plane] == float(c)
                        sat = jnp.where(same, table[0, c], sat)
                        shp = jnp.where(same, table[1, c] * LOG2E, shp)
                        cap = jnp.where(same, table[2, c], cap)
                    BIG[SAT, at, :] = sat
                    BIG[SHP, at, :] = shp
                    BIG[CAP, at, :] = cap
                    BIG[H, at, :] = heads[plane]

        ids = jnp.broadcast_to(cell[0], (LANES, n_emit))
        amount = jnp.broadcast_to(rate[0], (LANES, n_emit))
        column = lax.bitwise_and(ids, LANES - 1)
        line = lax.rem(lax.shift_right_logical(ids, 7), rows)
        layer = lax.div(lax.shift_right_logical(ids, 7), rows)
        wanted_lane = lax.bitwise_and(column, LANES - 8) + lax.div(line, XI)
        plane_row = lax.bitwise_and(column, 7) * XI + lax.rem(line, XI) + layer * rows
        here = wanted_lane == lax.broadcasted_iota(jnp.int32, (LANES, n_emit), 0)
        picked = jnp.where(here, amount, 0.0)
        part0 = picked.astype(jnp.bfloat16)
        rest = picked - part0.astype(jnp.float32)
        part1 = rest.astype(jnp.bfloat16)
        part2 = (rest - part1.astype(jnp.float32)).astype(jnp.bfloat16)

        @pl.loop(0, layers)
        def _(z):
            size = min(LANES, rows)
            for r in range(0, rows, size):
                wanted = lax.broadcasted_iota(jnp.int32, (size, n_emit), 0) + (z * rows + r)
                hot = jnp.where(plane_row[:size] == wanted, 1.0, 0.0).astype(jnp.bfloat16)
                total = jnp.zeros((size, LANES), jnp.float32)
                for part in (part2, part1, part0):
                    total = total + lax.dot_general(
                        hot, part, (((1,), (1,)), ((), ())), preferred_element_type=jnp.float32
                    )
                for s in range(0, size, XI):
                    plane = (r + s) // XI
                    at = pl.multiple_of((z + 1) * ZP + soil_row(plane, 0), 8)
                    BIG[EM, pl.ds(at, XI), :] = total[s : s + XI]

        @pl.loop(0, 5)
        def _(k):
            soil_out(jnp.where(k == 0, 0, k + 1), k)

        start(soil_copies(0))

        pltpu.make_async_copy(A_RECV, A_RECV, a_recv).wait()

        @pl.loop(0, 4)
        def _(n):
            field = jnp.where(n == 0, 0, n + 1)
            for q in range(nq):
                parts = fold([A_RECV[n, pl.ds(i * XI + 8 * q, 8), :] for i in range(8)])
                for plane in range(PLANES):
                    SF[field, pl.ds(film_row(plane, 8 * q), 8), :] = parts[plane]

        D, ELEV, GAIN, RAIN = 0, 2, 3, 4

        @pl.loop(0, 4)
        def _(k):
            surface_out(jnp.where(k == 0, 0, k + 1), k)

        start(surface_copies(0))
        wait_recv(soil_copies(0))

        @pl.loop(0, 5)
        def _(k):
            soil_in(jnp.where(k == 0, 0, k + 1), k)

        wait_recv(surface_copies(0))

        @pl.loop(0, 4)
        def _(k):
            surface_in(jnp.where(k == 0, 0, k + 1), k)

        def zbase(z):
            return pl.multiple_of((z + 1) * ZP, 8)

        @pl.loop(0, ROUNDS)
        def _(p):
            slot = lax.rem(p, 2)
            other = 1 - slot
            src = BIG.at[slot]
            dst = BIG.at[other]
            depth = SF.at[slot]

            @pl.when(p > 0)
            def _():
                wait_recv(soil_copies(p))
                soil_in(slot, 4 + p)
                wait_recv(surface_copies(p))
                surface_in(slot, 3 + p)

            @pl.loop(0, layers)
            def _(z):
                base = zbase(z)
                for plane in range(-2, PLANES + 2):
                    at = pl.ds(base + soil_row(plane, -2), N)
                    grow = jnp.exp2(BIG[SHP, at, :] * jnp.minimum(src[at, :], 0.0))
                    K[at, :] = BIG[SAT, at, :] * grow
                    if -2 < plane < PLANES + 1:
                        store = BIG[CAP, at, :] * grow + STORAGE
                        C[at, :] = store
                        B[at, :] = store * BIG[H, at, :] + BIG[EM, at, :]

            for plane in range(-3, PLANES + 3):
                at = pl.ds(film_row(plane, -3), N)
                d = depth[at, :]
                square = d * d + FILM_FLOOR
                FILM[at, :] = SF[GAIN, at, :] * (square * lax.rsqrt(square))
                ETA[at, :] = SF[ELEV, at, :] + d
            for plane in range(-3, PLANES + 2):
                at = pl.ds(film_row(plane, -3), N)
                film = FILM[at, :]
                GX[at, :] = film_face(film, FILM[pl.ds(film_row(plane, -2), N), :])
                GY[at, :] = film_face(film, FILM[pl.ds(film_row(plane + 1, -3), N), :])

            def film_sum(source, plane, first):
                at = pl.ds(film_row(plane, first), N)
                after = pl.ds(film_row(plane, first + 1), N)
                before = pl.ds(film_row(plane, first - 1), N)
                right = pl.ds(film_row(plane + 1, first), N)
                left = pl.ds(film_row(plane - 1, first), N)
                return (
                    SB[at, :]
                    + GX[at, :] * source[after, :]
                    + GX[before, :] * source[before, :]
                    + GY[at, :] * source[right, :]
                    + GY[left, :] * source[left, :]
                ) * SRD[at, :]

            high = (top + 1) * ZP
            for plane in range(-2, PLANES + 2):
                at = pl.ds(film_row(plane, -2), N)
                soil_at = pl.ds(high + soil_row(plane, -2), N)
                faces = (
                    GX[at, :]
                    + GX[pl.ds(film_row(plane, -3), N), :]
                    + GY[at, :]
                    + GY[pl.ds(film_row(plane - 1, -2), N), :]
                )
                cond = K[soil_at, :]
                start_level = SF[D, at, :] + SF[RAIN, at, :] + cond * src[soil_at, :]
                SB[at, :] = start_level - faces * SF[ELEV, at, :]
                SRD[at, :] = inverse(1.0 + cond + faces)
                ETA2[at, :] = film_sum(ETA, plane, -2) + SF[ELEV, at, :]
            for plane in range(-1, PLANES + 1):
                at = pl.ds(film_row(plane, -1), N)
                soil_at = pl.ds(high + soil_row(plane, -1), N)
                d = film_sum(ETA2, plane, -1)
                SF[other, at, :] = d
                B[soil_at, :] = B[soil_at, :] + K[soil_at, :] * (d - src[soil_at, :])

            @pl.when(p < ROUNDS - 1)
            def _():
                surface_out(other, 4 + p)
                start(surface_copies(p + 1))

            @pl.when(p == ROUNDS - 1)
            def _():
                for q in range(nq):
                    parts = fold([SF[D, pl.ds(film_row(i, 8 * q), 8), :] for i in range(8)])
                    for i in range(8):
                        DN[pl.ds(i * XI + 8 * q, 8), :] = parts[i]
                pltpu.make_async_copy(
                    DN.at[pl.ds(pl.multiple_of(t * 8, 8), 8), :],
                    depth_out.at[:, pl.ds(pl.multiple_of(t * LANES, LANES), LANES)],
                    o_recv,
                ).start()

                @pl.loop(1, n_tile)
                def _(d):
                    peer = lax.rem(t + d, n_tile)
                    pltpu.make_async_remote_copy(
                        src_ref=DN.at[pl.ds(pl.multiple_of(peer * 8, 8), 8), :],
                        dst_ref=depth_out.at[:, pl.ds(pl.multiple_of(t * LANES, LANES), LANES)],
                        send_sem=o_send,
                        recv_sem=o_recv,
                        device_id=(g, peer),
                        device_id_type=MESH,
                    ).start()

            @pl.loop(0, layers)
            def _(z):
                base = zbase(z)
                for plane in range(-2, PLANES + 1):
                    at = pl.ds(base + soil_row(plane, -1), N)
                    k = K[at, :]
                    FY[at, :] = face_of(k, K[pl.ds(base + soil_row(plane + 1, -1), N), :])
                    if plane > -2:
                        FZ[at, :] = face_of(k, K[pl.ds(base + ZP + soil_row(plane, -1), N), :])
                        before = pl.ds(base + soil_row(plane, -2), N)
                        FX[before, :] = face_of(K[before, :], k)

            def soil_sum(source, base, plane, first, size, at, value, below, above):
                after = pl.ds(base + soil_row(plane, first + 1), size)
                before = pl.ds(base + soil_row(plane, first - 1), size)
                right = pl.ds(base + soil_row(plane + 1, first), size)
                left = pl.ds(base + soil_row(plane - 1, first), size)
                return (
                    value
                    + FX[at, :] * source[after, :]
                    + FX[before, :] * source[before, :]
                    + FY[at, :] * source[right, :]
                    + FY[left, :] * source[left, :]
                    + above * source[pl.ds(base + ZP + soil_row(plane, first), size), :]
                    + below * source[pl.ds(base - ZP + soil_row(plane, first), size), :]
                )

            @pl.loop(0, layers)
            def _(z):
                base = zbase(z)
                for plane in range(-1, PLANES + 1):
                    at = pl.ds(base + soil_row(plane, -1), N)
                    below = FZ[pl.ds(base - ZP + soil_row(plane, -1), N), :]
                    above = FZ[at, :]
                    total = (
                        C[at, :]
                        + FX[at, :]
                        + FX[pl.ds(base + soil_row(plane, -2), N), :]
                        + FY[at, :]
                        + FY[pl.ds(base + soil_row(plane - 1, -1), N), :]
                        + above
                        + below
                    )
                    scale = inverse(total)
                    value = B[at, :] + (above - below)
                    RD[at, :] = scale
                    B[at, :] = value
                    total = soil_sum(src, base, plane, -1, N, at, value, below, above)
                    G1[at, :] = total * scale

            @pl.loop(0, layers)
            def _(z):
                base = zbase(z)
                for plane in range(PLANES):
                    at = pl.ds(base + soil_row(plane, 0), XI)
                    below = FZ[pl.ds(base - ZP + soil_row(plane, 0), XI), :]
                    total = soil_sum(
                        G1, base, plane, 0, XI, at, B[at, :], below, FZ[at, :]
                    )
                    dst[at, :] = total * RD[at, :]

            @pl.when(p < ROUNDS - 1)
            def _():
                soil_out(other, 5 + p)
                start(soil_copies(p + 1))

        @pl.loop(0, layers)
        def _(z):
            base = zbase(z)
            for q in range(nq):
                parts = fold([BIG[H, pl.ds(base + soil_row(i, 8 * q), 8), :] for i in range(8)])
                for i in range(8):
                    NAT[z, pl.ds(i * XI + 8 * q, 8), :] = parts[i]

        out = pltpu.make_async_copy(NAT, head_out, out_sem)
        out.start()

        wait_send(soil_copies(0))
        wait_send(surface_copies(0))

        @pl.loop(1, ROUNDS)
        def _(e):
            wait_send(soil_copies(e))
            wait_send(surface_copies(e))

        sent = A_SEND.at[:, :, pl.ds(0, (n_tile - 1) * LANES)]
        pltpu.make_async_copy(sent, sent, a_send).wait()
        gone = DN.at[pl.ds(0, (n_tile - 1) * 8), :]
        pltpu.make_async_copy(gone, gone, o_send).wait()
        pltpu.make_async_copy(depth_out, depth_out, o_recv).wait()
        out.wait()

    f32 = jnp.float32

    def vmem(*shape, dtype=f32):
        return pltpu.VMEM(shape, dtype)

    wide = n_tile * LANES
    dma = pltpu.SemaphoreType.DMA
    tall = (layers + 2) * ZP
    ks, kd = 5 + ROUNDS - 1, 4 + ROUNDS - 1
    scratch = [
        vmem(6, tall, LANES),
        vmem(tall, LANES),
        vmem(tall, LANES),
        vmem(tall, LANES),
        vmem(tall, LANES),
        vmem(tall, LANES),
        vmem(tall, LANES),
        vmem(tall, LANES),
        vmem(tall, LANES),
        vmem(layers, rows, LANES),
        vmem(layers, rows, LANES, dtype=jnp.int32),
        vmem(4, 8, wide),
        vmem(4, rows, LANES),
        vmem(8, wide),
        vmem(8, wide, dtype=jnp.int32),
        vmem(rows, LANES),
        vmem(5, SP, LANES),
        vmem(SP, LANES),
        vmem(SP, LANES),
        vmem(SP, LANES),
        vmem(SP, LANES),
        vmem(SP, LANES),
        vmem(SP, LANES),
        vmem(SP, LANES),
        vmem(ks, layers, 8, LANES),
        vmem(2, ks, layers, 8, LANES),
        vmem(ks, 4, 8, LANES),
        vmem(2, ks, 4, 8, LANES),
        vmem(4, ks, 8, LANES),
        vmem(4, ks, 8, LANES),
        vmem(kd, yv, 8, LANES),
        vmem(2, kd, yv, 8, LANES),
        vmem(kd, 8, LANES),
        vmem(2, kd, 8, LANES),
        vmem(4, kd, 8, LANES),
        vmem(4, kd, 8, LANES),
        dma((7,)), dma(()), dma(()), dma(()), dma(()), dma(()),
        dma((ROUNDS, 8)), dma((ROUNDS, 8)), dma((ROUNDS, 8)), dma((ROUNDS, 8)),
    ]
    anywhere = pl.BlockSpec(memory_space=pl.ANY)
    in_vmem = pl.BlockSpec(memory_space=pltpu.VMEM)
    return pl.pallas_call(
        kernel,
        out_shape=(
            jax.ShapeDtypeStruct((layers, rows, LANES), f32),
            jax.ShapeDtypeStruct((8, wide), f32),
        ),
        in_specs=[
            anywhere, anywhere, pl.BlockSpec(memory_space=pltpu.SMEM), in_vmem, in_vmem,
            anywhere, anywhere, anywhere, anywhere, anywhere,
        ],
        out_specs=(anywhere, anywhere),
        scratch_shapes=scratch,
        compiler_params=pltpu.CompilerParams(
            collective_id=0, has_side_effects=True, vmem_limit_bytes=60 * 1024 * 1024
        ),
    )


def solution(mesh):
    n_grp, n_tile = mesh.shape["grp"], mesh.shape["tile"]

    def shards(soil_head, soil_type, soil_table, emitter_cell, emitter_rate, *surface):
        layers, rows, _ = soil_head.shape
        run = make_kernel(
            n_grp, n_tile, layers, rows, soil_table.shape[1], emitter_cell.shape[-1]
        )
        return run(soil_head, soil_type, soil_table, emitter_cell, emitter_rate, *surface)

    cells = P(None, "grp", "tile")
    strip = P(("grp", "tile"), None)
    emitters = P("grp", "tile", None)
    return jax.shard_map(
        shards,
        mesh=mesh,
        in_specs=(cells, cells, P(), emitters, emitters, strip, strip, strip, strip, strip),
        out_specs=(cells, strip),
        check_vma=False,
    )
```

```python
import jax
import jax.numpy as jnp
from jax import lax
from jax.experimental import pallas as pl
from jax.experimental.pallas import tpu as pltpu
from jax.sharding import PartitionSpec as P

MESH = pl.DeviceIdType.MESH
STEPS = 2
PICARD = 2
ROUNDS = STEPS * PICARD
LANES = 128
STORAGE = 0.05
FILM_FLOOR = 0.04
BLEND = 0.05
LOG2E = 1.4426950408889634
OUTSIDE = 1e-30
PLANES = 8
WS, WD = 2, 3
H, SAT, SHP, CAP, EM = 0, 2, 3, 4, 5
SIDES = ((0, -1), (0, 1), (-1, 0), (1, 0), (1, 1), (1, -1), (-1, 1), (-1, -1))


def inverse(x):
    return pl.reciprocal(x, approx=True)


def face_of(a, b):
    return (a + a) * b * inverse(a + b)


def film_face(a, b):
    return (a + a) * b * inverse(a + b + BLEND)


def roll(x, shift):
    return pltpu.roll(x, shift % LANES, 1)


def make_kernel(n_grp, n_tile, layers, rows, n_types, n_emit):
    XI = rows // 8
    RP = XI + 16
    ZP = (PLANES + 2 * WS) * RP
    SP = (PLANES + 2 * WD) * RP
    nq = XI // 8
    top = layers - 1
    N = XI + 8
    yv = (WD * nq + 7) // 8

    def kernel(
        head_in, type_in, table, cell, rate, depth_in, elev_in, rough_in, pond_in, rain_in,
        head_out, depth_out,
        BIG, G1, K, FX, FY, FZ, RD, B, C, NAT, TYPE,
        A_SEND, A_RECV, ROUGH, POND, DN,
        SF, FILM, ETA, ETA2, GX, GY, SB, SRD,
        YS, YR, XS, XR, CS, CR, TYS, TYR, TXS, TXR, TCS, TCR,
        load_sem, a_send, a_recv, o_send, o_recv, out_sem,
        c_send, c_recv, t_send, t_recv,
    ):
        g = lax.axis_index("grp")
        t = lax.axis_index("tile")

        def inside(dg, dt):
            ok = jnp.bool_(True)
            if dg:
                ok = g + dg >= 0 if dg < 0 else g + dg < n_grp
            if dt:
                side = t + dt >= 0 if dt < 0 else t + dt < n_tile
                ok = jnp.logical_and(ok, side) if dg else side
            return ok

        has = [inside(dg, dt) for dg, dt in SIDES]
        came = [inside(-dg, -dt) for dg, dt in SIDES]
        target = [(g + dg, t + dt) for dg, dt in SIDES]

        loads = [
            pltpu.make_async_copy(rough_in, ROUGH, load_sem.at[0]),
            pltpu.make_async_copy(pond_in, POND, load_sem.at[1]),
            pltpu.make_async_copy(depth_in, A_SEND.at[0], load_sem.at[2]),
            pltpu.make_async_copy(elev_in, A_SEND.at[1], load_sem.at[3]),
            pltpu.make_async_copy(rain_in, A_SEND.at[3], load_sem.at[4]),
            pltpu.make_async_copy(type_in, TYPE, load_sem.at[5]),
            pltpu.make_async_copy(head_in, NAT, load_sem.at[6]),
        ]
        for copy in loads:
            copy.start()

        barrier = pltpu.get_barrier_semaphore()

        @pl.loop(1, n_tile)
        def _(d):
            pl.semaphore_signal(
                barrier, inc=1, device_id=(g, lax.rem(t + d, n_tile)), device_id_type=MESH
            )

        for side in range(2, 8):

            @pl.when(has[side])
            def _():
                pl.semaphore_signal(barrier, inc=1, device_id=target[side], device_id_type=MESH)

        lane = lax.broadcasted_iota(jnp.int32, (8, LANES), 1)
        xb = lax.bitwise_and(lane, 7)
        zero8 = jnp.zeros((8, LANES), jnp.float32)

        @pl.loop(0, ZP // 8)
        def _(r):
            for base in (0, (layers + 1) * ZP):
                at = pl.ds(pl.multiple_of(base + r * 8, 8), 8)
                BIG[H, at, :] = zero8
                BIG[H + 1, at, :] = zero8
                G1[at, :] = zero8
                K[at, :] = zero8
            FZ[pl.ds(pl.multiple_of(r * 8, 8), 8), :] = zero8

        for side in range(8):

            @pl.when(jnp.logical_not(came[side]))
            def _():
                for k in range(5 + ROUNDS - 1):
                    fill = zero8 + OUTSIDE if k == 1 else zero8
                    if side < 2:
                        for z in range(layers):
                            YR[side, k, z] = fill
                    elif side < 4:
                        for v in range(4):
                            XR[side - 2, k, v] = fill
                    else:
                        CR[side - 4, k] = fill
                for k in range(4 + ROUNDS - 1):
                    if side < 2:
                        for v in range(yv):
                            TYR[side, k, v] = zero8
                    elif side < 4:
                        TXR[side - 2, k] = zero8
                    else:
                        TCR[side - 4, k] = zero8

        def copies(bufs, k, count, send, recv):
            y_out, y_in, x_out, x_in, c_out, c_in = bufs
            at = pl.ds(k, count)
            out = []
            for side in range(8):
                if side < 2:
                    src, dst = y_out.at[at], y_in.at[side, at]
                elif side < 4:
                    src, dst = x_out.at[at], x_in.at[side - 2, at]
                else:
                    src, dst = c_out.at[side - 4, at], c_in.at[side - 4, at]
                out.append(
                    pltpu.make_async_remote_copy(
                        src_ref=src,
                        dst_ref=dst,
                        send_sem=send.at[side],
                        recv_sem=recv.at[side],
                        device_id=target[side],
                        device_id_type=MESH,
                    )
                )
            return out

        soil_bufs = (YS, YR, XS, XR, CS, CR)
        surface_bufs = (TYS, TYR, TXS, TXR, TCS, TCR)

        def soil_copies(e):
            if isinstance(e, int) and e == 0:
                return copies(soil_bufs, 0, 5, c_send.at[0], c_recv.at[0])
            return copies(soil_bufs, 4 + e, 1, c_send.at[e], c_recv.at[e])

        def surface_copies(e):
            if isinstance(e, int) and e == 0:
                return copies(surface_bufs, 0, 4, t_send.at[0], t_recv.at[0])
            return copies(surface_bufs, 3 + e, 1, t_send.at[e], t_recv.at[e])

        def start(made):
            for side in (1, 0, 4, 5, 6, 7, 2, 3):

                @pl.when(has[side])
                def _():
                    made[side].start()

        def wait_recv(made):
            for side in range(8):

                @pl.when(came[side])
                def _():
                    made[side].wait_recv()

        def wait_send(made):
            for side in range(8):

                @pl.when(has[side])
                def _():
                    made[side].wait_send()

        def fold(v):
            v = list(v)
            for k in (1, 2, 4):
                low = lax.bitwise_and(lane, k) == 0
                for a in range(8):
                    if a & k == 0:
                        p, q = v[a], v[a | k]
                        v[a] = jnp.where(low, p, roll(q, k))
                        v[a | k] = jnp.where(low, roll(p, -k), q)
            return v

        def zbase(z):
            return pl.multiple_of((z + 1) * ZP, 8)

        def soil_row(plane, xi):
            return (plane + WS) * RP + 8 + xi

        def film_row(plane, xi):
            return (plane + WD) * RP + 8 + xi

        def columns_out(R, row, width, jobs):
            spots = [(a, q) for a in range(1, width + 1) for q in range(nq)]
            read = []
            for base, put, values in jobs:
                for a, q in spots:
                    if values is None:
                        high = R[pl.ds(base + row(PLANES - a, 8 * q), 8), :]
                        low = R[pl.ds(base + row(a - 1, 8 * q), 8), :]
                    else:
                        high = values[PLANES - a][8 * q : 8 * q + 8]
                        low = values[a - 1][8 * q : 8 * q + 8]
                    read.append((high, low))
            moved = [(roll(high, 8), roll(low, -8)) for high, low in read]
            packs = []
            for n in range(len(jobs)):
                packed = zero8
                for i in range(len(spots)):
                    high, low = moved[n * len(spots) + i]
                    both = roll(jnp.where(lane >= LANES // 2, low, high), 16 * (i % 8) + 8)
                    packed = jnp.where(lax.shift_right_logical(lane, 4) == i % 8, both, packed)
                    if i % 8 == 7 or i == len(spots) - 1:
                        packs.append((n, i // 8, packed))
                        packed = zero8
            for n, (base, put, values) in enumerate(jobs):
                for i, (a, q) in enumerate(spots):
                    high, low = moved[n * len(spots) + i]
                    R[pl.ds(base + row(-a, 8 * q), 8), :] = high
                    R[pl.ds(base + row(PLANES - 1 + a, 8 * q), 8), :] = low
            for n, v, packed in packs:
                jobs[n][1](v, packed)

        def columns_in(R, row, width, jobs):
            spots = [(a, q) for a in range(1, width + 1) for q in range(nq)]
            todo = []
            for base, get in jobs:
                for i, (a, q) in enumerate(spots):
                    if i % 8 == 0:
                        from_right, from_left = get(i // 8)
                        met = jnp.where(lax.bitwise_and(lane, 15) < 8, from_right, from_left)
                    left = pl.ds(base + row(-a, 8 * q), 8)
                    right = pl.ds(base + row(PLANES - 1 + a, 8 * q), 8)
                    u = roll(met, -(16 * (i % 8) + 8))
                    todo.append((left, right, u, R[left, :], R[right, :]))
            for left, right, u, was_left, was_right in todo:
                R[left, :] = jnp.where(lane < 8, u, was_left)
                R[right, :] = jnp.where(lane >= LANES - 8, u, was_right)

        def rows_out(R, row, jobs, packs):
            read = []
            for base, b, slot, v in jobs:
                high = R[pl.ds(base + row(0, XI - b), 8, stride=RP), :]
                low = R[pl.ds(base + row(0, b - 1), 8, stride=RP), :]
                read.append((roll(high, 1), roll(low, -1)))
            for (base, b, slot, v), (high, low) in zip(jobs, read):
                both = roll(jnp.where(xb == 7, low, high), 2 * slot + 1)
                mine = lax.shift_right_logical(xb, 1) == slot
                packs[v] = jnp.where(mine, both, packs[v])
            for (base, b, slot, v), (high, low) in zip(jobs, read):
                R[pl.ds(base + row(0, -b), 8, stride=RP), :] = high
                R[pl.ds(base + row(0, XI - 1 + b), 8, stride=RP), :] = low

        def rows_meet(from_down, from_up):
            return jnp.where(lax.bitwise_and(lane, 1) == 1, roll(from_up, -8), roll(from_down, 8))

        def rows_in(R, row, jobs, met):
            todo = []
            for base, b, slot, v in jobs:
                up = pl.ds(base + row(0, -b), 8, stride=RP)
                down = pl.ds(base + row(0, XI - 1 + b), 8, stride=RP)
                todo.append((up, down, roll(met[v], -(2 * slot + 1)), R[up, :], R[down, :]))
            for up, down, u, was_up, was_down in todo:
                R[up, :] = jnp.where(xb == 0, u, was_up)
                R[down, :] = jnp.where(xb == 7, u, was_down)

        def corner_source(gather, side, a, b):
            plane = PLANES - a if side in (4, 6) else a - 1
            xi = XI - b if side in (4, 5) else b - 1
            return roll(gather(plane, xi), {4: 1, 5: 113, 6: 15, 7: 127}[side])

        def corner_value(gather, side, a, b, diagonal):
            ln = lane[: diagonal.shape[0]]
            x8 = xb[: diagonal.shape[0]]
            first = side in (4, 6)
            plane = -a if first else PLANES - 1 + a
            if side in (4, 5):
                inner = roll(gather(plane, XI - b), 1)
                other = gather(PLANES - a if first else a - 1, -b)
                near = x8 > 0
            else:
                inner = roll(gather(plane, b - 1), -1)
                other = gather(PLANES - a if first else a - 1, XI - 1 + b)
                near = x8 < 7
            other = roll(other, 8 if first else -8)
            known = ln >= 8 if first else ln < LANES - 8
            return jnp.where(near, inner, jnp.where(known, other, diagonal))

        def corner_place(side, a, b):
            return -a if side in (4, 6) else PLANES - 1 + a, -b if side in (4, 5) else XI - 1 + b

        def soil_put(k, z):
            def put(v, value):
                YS[k, z] = value

            return put

        def soil_jobs(width):
            return [
                ((z + 1) * ZP, b, z % 4, (b - 1) * 2 + z // 4)
                for z in range(layers)
                for b in range(1, width + 1)
            ]

        def soil_rows_out(f, k, width):
            R = BIG.at[f]
            packs = [zero8] * 4
            rows_out(R, soil_row, soil_jobs(width), packs)
            for v in range(4):
                XS[k, v] = packs[v]

            def gather(plane, xi):
                return R[pl.ds(ZP + soil_row(plane, xi), layers, stride=ZP), :]

            for side in range(4, 8):
                CS[side - 4, k] = corner_source(gather, side, 1, 1)

        def soil_in(f, k, width):
            R = BIG.at[f]

            @pl.loop(0, layers // 4)
            def _(h):
                columns_in(
                    R, soil_row, width,
                    [
                        (zbase(4 * h + n), lambda v, z=4 * h + n: (YR[0, k, z], YR[1, k, z]))
                        for n in range(4)
                    ],
                )

            met = [rows_meet(XR[0, k, v], XR[1, k, v]) for v in range(4)]
            rows_in(R, soil_row, soil_jobs(width), met)

            def gather(plane, xi):
                return R[pl.ds(ZP + soil_row(plane, xi), layers, stride=ZP), :]

            for side in range(4, 8):
                value = corner_value(gather, side, 1, 1, CR[side - 4, k])
                plane, xi = corner_place(side, 1, 1)
                R[pl.ds(ZP + soil_row(plane, xi), layers, stride=ZP), :] = value

        corners = ((1, 1), (1, 2), (2, 1))

        def surface_out(f, k):
            R = SF.at[f]

            def put(v, value):
                TYS[k, v] = value

            columns_out(R, film_row, WD, [(0, put, None)])
            packs = [zero8]
            rows_out(R, film_row, [(0, b, b - 1, 0) for b in range(1, WD + 1)], packs)
            TXS[k] = packs[0]

            def gather(plane, xi):
                return R[pl.ds(film_row(plane, xi), 1), :]

            for side in range(4, 8):
                for n, (a, b) in enumerate(corners):
                    TCS[side - 4, k, pl.ds(n, 1), :] = corner_source(gather, side, a, b)

        def surface_in(f, k):
            R = SF.at[f]
            columns_in(R, film_row, WD, [(0, lambda v: (TYR[0, k, v], TYR[1, k, v]))])
            met = [rows_meet(TXR[0, k], TXR[1, k])]
            rows_in(R, film_row, [(0, b, b - 1, 0) for b in range(1, WD + 1)], met)

            def gather(plane, xi):
                return R[pl.ds(film_row(plane, xi), 1), :]

            for side in range(4, 8):
                for n, (a, b) in enumerate(corners):
                    value = corner_value(gather, side, a, b, TCR[side - 4, k, pl.ds(n, 1), :])
                    plane, xi = corner_place(side, a, b)
                    R[pl.ds(film_row(plane, xi), 1), :] = value

        @pl.loop(0, 4 + ROUNDS - 1)
        def _(k):
            for side in range(4):
                TCS[side, k] = zero8

        loads[5].wait()
        loads[6].wait()

        @pl.loop(0, layers)
        def _(z):
            base = (z + 1) * ZP
            for q in range(nq):
                kinds = fold(
                    [TYPE[z, pl.ds(i * XI + 8 * q, 8), :].astype(jnp.float32) for i in range(8)]
                )
                heads = fold([NAT[z, pl.ds(i * XI + 8 * q, 8), :] for i in range(8)])
                for plane in range(PLANES):
                    at = pl.ds(pl.multiple_of(base + soil_row(plane, 8 * q), 8), 8)
                    sat = shp = cap = zero8
                    for c in range(n_types):
                        same = kinds[plane] == float(c)
                        sat = jnp.where(same, table[0, c], sat)
                        shp = jnp.where(same, table[1, c] * LOG2E, shp)
                        cap = jnp.where(same, table[2, c], cap)
                    BIG[SAT, at, :] = sat
                    BIG[SHP, at, :] = shp
                    BIG[CAP, at, :] = cap
                    BIG[H, at, :] = heads[plane]

        ids = jnp.broadcast_to(cell[0], (LANES, n_emit))
        amount = jnp.broadcast_to(rate[0], (LANES, n_emit))
        column = lax.bitwise_and(ids, LANES - 1)
        line = lax.rem(lax.shift_right_logical(ids, 7), rows)
        layer = lax.div(lax.shift_right_logical(ids, 7), rows)
        wanted_lane = lax.bitwise_and(column, LANES - 8) + lax.div(line, XI)
        plane_row = lax.bitwise_and(column, 7) * XI + lax.rem(line, XI) + layer * rows
        here = wanted_lane == lax.broadcasted_iota(jnp.int32, (LANES, n_emit), 0)
        picked = jnp.where(here, amount, 0.0)
        part0 = picked.astype(jnp.bfloat16)
        rest = picked - part0.astype(jnp.float32)
        part1 = rest.astype(jnp.bfloat16)
        part2 = (rest - part1.astype(jnp.float32)).astype(jnp.bfloat16)

        @pl.loop(0, layers)
        def _(z):
            size = min(LANES, rows)
            for r in range(0, rows, size):
                wanted = lax.broadcasted_iota(jnp.int32, (size, n_emit), 0) + (z * rows + r)
                hot = jnp.where(plane_row[:size] == wanted, 1.0, 0.0).astype(jnp.bfloat16)
                total = jnp.zeros((size, LANES), jnp.float32)
                for part in (part2, part1, part0):
                    total = total + lax.dot_general(
                        hot, part, (((1,), (1,)), ((), ())), preferred_element_type=jnp.float32
                    )
                for s in range(0, size, XI):
                    plane = (r + s) // XI
                    at = pl.multiple_of((z + 1) * ZP + soil_row(plane, 0), 8)
                    BIG[EM, pl.ds(at, XI), :] = total[s : s + XI]

        for copy in loads[:5]:
            copy.wait()
        A_SEND[2] = ROUGH[...] * POND[...].astype(jnp.float32)
        own = pltpu.make_async_copy(
            A_SEND.at[:, :, pl.ds(pl.multiple_of(t * LANES, LANES), LANES)],
            A_RECV.at[:, pl.ds(pl.multiple_of(t * 8, 8), 8), :],
            a_recv,
        )
        own.start()

        beside = jnp.int32(0)
        for side in range(2, 8):
            beside = beside + came[side].astype(jnp.int32)
        pl.semaphore_wait(barrier, n_tile - 1 + beside)

        @pl.loop(1, n_tile)
        def _(d):
            peer = lax.rem(t + d, n_tile)
            pltpu.make_async_remote_copy(
                src_ref=A_SEND.at[:, :, pl.ds(pl.multiple_of(peer * LANES, LANES), LANES)],
                dst_ref=A_RECV.at[:, pl.ds(pl.multiple_of(t * 8, 8), 8), :],
                send_sem=a_send,
                recv_sem=a_recv,
                device_id=(g, peer),
                device_id_type=MESH,
            ).start()

        for first, last, width in ((0, 3, WS), (3, 5, 1)):

            @pl.loop(first, last)
            def _(k):
                field = jnp.where(k == 0, 0, k + 1)

                @pl.loop(0, layers // 2)
                def _(h):
                    columns_out(
                        BIG.at[field], soil_row, width,
                        [(zbase(2 * h + n), soil_put(k, 2 * h + n), None) for n in range(2)],
                    )

                soil_rows_out(field, k, width)

        start(soil_copies(0))

        D, ELEV, GAIN, RAIN = 0, 2, 3, 4

        @pl.loop(0, ROUNDS)
        def _(p):
            slot = lax.rem(p, 2)
            other = 1 - slot
            src = BIG.at[slot]
            dst = BIG.at[other]
            depth = SF.at[slot]

            def react(at, base_too):
                grow = jnp.exp2(BIG[SHP, at, :] * jnp.minimum(src[at, :], 0.0))
                K[at, :] = BIG[SAT, at, :] * grow
                if base_too:
                    store = BIG[CAP, at, :] * grow + STORAGE
                    C[at, :] = store
                    B[at, :] = store * BIG[H, at, :] + BIG[EM, at, :]

            @pl.loop(0, layers)
            def _(z):
                base = zbase(z)
                for plane in range(PLANES):
                    react(pl.ds(base + soil_row(plane, 0), XI), True)

            @pl.loop(0, layers)
            def _(z):
                base = zbase(z)
                for plane in range(PLANES):
                    at = pl.ds(base + soil_row(plane, 0), XI)
                    k = K[at, :]
                    FX[at, :] = face_of(k, K[pl.ds(base + soil_row(plane, 1), XI), :])
                    FZ[at, :] = face_of(k, K[pl.ds(base + ZP + soil_row(plane, 0), XI), :])
                    if plane < PLANES - 1:
                        FY[at, :] = face_of(k, K[pl.ds(base + soil_row(plane + 1, 0), XI), :])

            def first_at(base, plane, xi, size, stride=None):
                def spot(dz=0, dp=0, dx=0):
                    return pl.ds(base + dz * ZP + soil_row(plane + dp, xi + dx), size, stride=stride)

                at, before, left, down = spot(), spot(dx=-1), spot(dp=-1), spot(dz=-1)
                fx, fxm, fy, fym = FX[at, :], FX[before, :], FY[at, :], FY[left, :]
                above, below = FZ[at, :], FZ[down, :]
                scale = inverse(C[at, :] + fx + fxm + fy + fym + above + below)
                RD[at, :] = scale
                total = (
                    B[at, :]
                    + (above - below)
                    + fx * src[spot(dx=1), :]
                    + fxm * src[before, :]
                    + fy * src[spot(dp=1), :]
                    + fym * src[left, :]
                    + above * src[spot(dz=1), :]
                    + below * src[down, :]
                )
                G1[at, :] = total * scale

            def first_outer(base):
                for plane in (-1, 0, PLANES - 1, PLANES):
                    first_at(base, plane, -1, N)
                for xi in (-1, 0, XI - 1, XI):
                    first_at(base, 0, xi, 8, RP)

            @pl.loop(0, top)
            def _(z):
                for plane in range(1, PLANES - 1):
                    first_at(zbase(z), plane, 0, XI)

            @pl.when(p == 0)
            def _():
                pltpu.make_async_copy(A_RECV, A_RECV, a_recv).wait()

                @pl.loop(0, 4)
                def _(n):
                    field = jnp.where(n == 0, 0, n + 1)
                    for q in range(nq):
                        parts = fold([A_RECV[n, pl.ds(i * XI + 8 * q, 8), :] for i in range(8)])
                        for plane in range(PLANES):
                            SF[field, pl.ds(film_row(plane, 8 * q), 8), :] = parts[plane]

                @pl.loop(0, 4)
                def _(k):
                    surface_out(jnp.where(k == 0, 0, k + 1), k)

                start(surface_copies(0))
                wait_recv(soil_copies(0))

                for first, last, width in ((0, 3, WS), (3, 5, 1)):

                    @pl.loop(first, last)
                    def _(k):
                        soil_in(jnp.where(k == 0, 0, k + 1), k, width)

            @pl.when(p > 0)
            def _():
                wait_recv(soil_copies(p))
                soil_in(slot, 4 + p, WS)

            def line(base, plane, xi):
                return pl.ds(base + soil_row(plane, xi), 8, stride=RP)

            @pl.loop(0, layers)
            def _(z):
                base = zbase(z)
                for plane in (-2, -1, PLANES, PLANES + 1):
                    react(pl.ds(base + soil_row(plane, -2), N), plane in (-1, PLANES))
                for xi in (-2, -1, XI, XI + 1):
                    react(line(base, 0, xi), xi in (-1, XI))

            @pl.loop(0, layers)
            def _(z):
                base = zbase(z)
                for plane in (-2, -1, PLANES - 1, PLANES):
                    at = pl.ds(base + soil_row(plane, -1), N)
                    k = K[at, :]
                    FY[at, :] = face_of(k, K[pl.ds(base + soil_row(plane + 1, -1), N), :])
                    if plane in (-1, PLANES):
                        FZ[at, :] = face_of(k, K[pl.ds(base + ZP + soil_row(plane, -1), N), :])
                        before = pl.ds(base + soil_row(plane, -2), N)
                        FX[before, :] = face_of(K[before, :], k)
                for xi in (-2, -1, XI - 1, XI):
                    at = line(base, 0, xi)
                    k = K[at, :]
                    FX[at, :] = face_of(k, K[line(base, 0, xi + 1), :])
                    if xi in (-1, XI):
                        FZ[at, :] = face_of(k, K[line(base + ZP, 0, xi), :])
                        FY[at, :] = face_of(k, K[line(base, 1, xi), :])

            early = jnp.where(p < ROUNDS - 1, top, 0)

            @pl.loop(0, early)
            def _(z):
                first_outer(zbase(z))

            @pl.when(p == 0)
            def _():
                wait_recv(surface_copies(0))

                @pl.loop(0, 4)
                def _(k):
                    surface_in(jnp.where(k == 0, 0, k + 1), k)

            @pl.when(p > 0)
            def _():
                wait_recv(surface_copies(p))
                surface_in(slot, 3 + p)

            for plane in range(-3, PLANES + 3):
                at = pl.ds(film_row(plane, -3), N)
                d = depth[at, :]
                square = d * d + FILM_FLOOR
                FILM[at, :] = SF[GAIN, at, :] * (square * lax.rsqrt(square))
                ETA[at, :] = SF[ELEV, at, :] + d
            for plane in range(-3, PLANES + 2):
                at = pl.ds(film_row(plane, -3), N)
                film = FILM[at, :]
                GX[at, :] = film_face(film, FILM[pl.ds(film_row(plane, -2), N), :])
                GY[at, :] = film_face(film, FILM[pl.ds(film_row(plane + 1, -3), N), :])

            def film_sum(source, plane, first):
                at = pl.ds(film_row(plane, first), N)
                after = pl.ds(film_row(plane, first + 1), N)
                before = pl.ds(film_row(plane, first - 1), N)
                right = pl.ds(film_row(plane + 1, first), N)
                left = pl.ds(film_row(plane - 1, first), N)
                return (
                    SB[at, :]
                    + GX[at, :] * source[after, :]
                    + GX[before, :] * source[before, :]
                    + GY[at, :] * source[right, :]
                    + GY[left, :] * source[left, :]
                ) * SRD[at, :]

            high = (top + 1) * ZP
            for plane in range(-2, PLANES + 2):
                at = pl.ds(film_row(plane, -2), N)
                soil_at = pl.ds(high + soil_row(plane, -2), N)
                faces = (
                    GX[at, :]
                    + GX[pl.ds(film_row(plane, -3), N), :]
                    + GY[at, :]
                    + GY[pl.ds(film_row(plane - 1, -2), N), :]
                )
                cond = K[soil_at, :]
                start_level = SF[D, at, :] + SF[RAIN, at, :] + cond * src[soil_at, :]
                SB[at, :] = start_level - faces * SF[ELEV, at, :]
                SRD[at, :] = inverse(1.0 + cond + faces)
                ETA2[at, :] = film_sum(ETA, plane, -2) + SF[ELEV, at, :]
            for plane in range(-1, PLANES + 1):
                at = pl.ds(film_row(plane, -1), N)
                soil_at = pl.ds(high + soil_row(plane, -1), N)
                d = film_sum(ETA2, plane, -1)
                SF[other, at, :] = d
                B[soil_at, :] = B[soil_at, :] + K[soil_at, :] * (d - src[soil_at, :])

            @pl.when(p < ROUNDS - 1)
            def _():
                surface_out(other, 4 + p)
                start(surface_copies(p + 1))

            @pl.when(p == ROUNDS - 1)
            def _():
                for q in range(nq):
                    parts = fold([SF[D, pl.ds(film_row(i, 8 * q), 8), :] for i in range(8)])
                    for i in range(8):
                        DN[pl.ds(i * XI + 8 * q, 8), :] = parts[i]
                pltpu.make_async_copy(
                    DN.at[pl.ds(pl.multiple_of(t * 8, 8), 8), :],
                    depth_out.at[:, pl.ds(pl.multiple_of(t * LANES, LANES), LANES)],
                    o_recv,
                ).start()

                @pl.loop(1, n_tile)
                def _(d):
                    peer = lax.rem(t + d, n_tile)
                    pltpu.make_async_remote_copy(
                        src_ref=DN.at[pl.ds(pl.multiple_of(peer * 8, 8), 8), :],
                        dst_ref=depth_out.at[:, pl.ds(pl.multiple_of(t * LANES, LANES), LANES)],
                        send_sem=o_send,
                        recv_sem=o_recv,
                        device_id=(g, peer),
                        device_id_type=MESH,
                    ).start()

            def soil_sum(source, base, plane, first, size, at, value, below, above):
                after = pl.ds(base + soil_row(plane, first + 1), size)
                before = pl.ds(base + soil_row(plane, first - 1), size)
                right = pl.ds(base + soil_row(plane + 1, first), size)
                left = pl.ds(base + soil_row(plane - 1, first), size)
                return (
                    value
                    + FX[at, :] * source[after, :]
                    + FX[before, :] * source[before, :]
                    + FY[at, :] * source[right, :]
                    + FY[left, :] * source[left, :]
                    + above * source[pl.ds(base + ZP + soil_row(plane, first), size), :]
                    + below * source[pl.ds(base - ZP + soil_row(plane, first), size), :]
                )

            @pl.loop(early, top)
            def _(z):
                first_outer(zbase(z))

            for plane in range(-1, PLANES + 1):
                first_at(high, plane, -1, N)

            def second_sweep(base):
                values = []
                for plane in range(PLANES):
                    at = pl.ds(base + soil_row(plane, 0), XI)
                    below = FZ[pl.ds(base - ZP + soil_row(plane, 0), XI), :]
                    total = soil_sum(
                        G1, base, plane, 0, XI, at, B[at, :] + (FZ[at, :] - below), below, FZ[at, :]
                    )
                    values.append(total * RD[at, :])
                    dst[at, :] = values[-1]
                return values

            @pl.when(p < ROUNDS - 1)
            def _():
                @pl.loop(0, layers)
                def _(z):
                    base = zbase(z)
                    values = second_sweep(base)
                    columns_out(dst, soil_row, WS, [(base, soil_put(5 + p, z), values)])

                soil_rows_out(other, 5 + p, WS)
                start(soil_copies(p + 1))

            @pl.when(p == ROUNDS - 1)
            def _():
                @pl.loop(0, layers)
                def _(z):
                    base = zbase(z)
                    values = second_sweep(base)
                    for q in range(nq):
                        parts = fold([values[i][8 * q : 8 * q + 8] for i in range(8)])
                        for i in range(8):
                            NAT[z, pl.ds(i * XI + 8 * q, 8), :] = parts[i]
                    pltpu.make_async_copy(NAT.at[z], head_out.at[z], out_sem).start()

        wait_send(soil_copies(0))
        wait_send(surface_copies(0))

        @pl.loop(1, ROUNDS)
        def _(e):
            wait_send(soil_copies(e))
            wait_send(surface_copies(e))

        sent = A_SEND.at[:, :, pl.ds(0, (n_tile - 1) * LANES)]
        pltpu.make_async_copy(sent, sent, a_send).wait()
        gone = DN.at[pl.ds(0, (n_tile - 1) * 8), :]
        pltpu.make_async_copy(gone, gone, o_send).wait()
        pltpu.make_async_copy(depth_out, depth_out, o_recv).wait()
        pltpu.make_async_copy(NAT, head_out, out_sem).wait()

    f32 = jnp.float32

    def vmem(*shape, dtype=f32):
        return pltpu.VMEM(shape, dtype)

    wide = n_tile * LANES
    dma = pltpu.SemaphoreType.DMA
    tall = (layers + 2) * ZP
    ks, kd = 5 + ROUNDS - 1, 4 + ROUNDS - 1
    scratch = [
        vmem(6, tall, LANES),
        vmem(tall, LANES),
        vmem(tall, LANES),
        vmem(tall, LANES),
        vmem(tall, LANES),
        vmem(tall, LANES),
        vmem(tall, LANES),
        vmem(tall, LANES),
        vmem(tall, LANES),
        vmem(layers, rows, LANES),
        vmem(layers, rows, LANES, dtype=jnp.int32),
        vmem(4, 8, wide),
        vmem(4, rows, LANES),
        vmem(8, wide),
        vmem(8, wide, dtype=jnp.int32),
        vmem(rows, LANES),
        vmem(5, SP, LANES),
        vmem(SP, LANES),
        vmem(SP, LANES),
        vmem(SP, LANES),
        vmem(SP, LANES),
        vmem(SP, LANES),
        vmem(SP, LANES),
        vmem(SP, LANES),
        vmem(ks, layers, 8, LANES),
        vmem(2, ks, layers, 8, LANES),
        vmem(ks, 4, 8, LANES),
        vmem(2, ks, 4, 8, LANES),
        vmem(4, ks, 8, LANES),
        vmem(4, ks, 8, LANES),
        vmem(kd, yv, 8, LANES),
        vmem(2, kd, yv, 8, LANES),
        vmem(kd, 8, LANES),
        vmem(2, kd, 8, LANES),
        vmem(4, kd, 8, LANES),
        vmem(4, kd, 8, LANES),
        dma((7,)), dma(()), dma(()), dma(()), dma(()), dma(()),
        dma((ROUNDS, 8)), dma((ROUNDS, 8)), dma((ROUNDS, 8)), dma((ROUNDS, 8)),
    ]
    anywhere = pl.BlockSpec(memory_space=pl.ANY)
    in_vmem = pl.BlockSpec(memory_space=pltpu.VMEM)
    return pl.pallas_call(
        kernel,
        out_shape=(
            jax.ShapeDtypeStruct((layers, rows, LANES), f32),
            jax.ShapeDtypeStruct((8, wide), f32),
        ),
        in_specs=[
            anywhere, anywhere, pl.BlockSpec(memory_space=pltpu.SMEM), in_vmem, in_vmem,
            anywhere, anywhere, anywhere, anywhere, anywhere,
        ],
        out_specs=(anywhere, anywhere),
        scratch_shapes=scratch,
        compiler_params=pltpu.CompilerParams(
            collective_id=0, has_side_effects=True, vmem_limit_bytes=60 * 1024 * 1024
        ),
    )


def solution(mesh):
    n_grp, n_tile = mesh.shape["grp"], mesh.shape["tile"]

    def shards(soil_head, soil_type, soil_table, emitter_cell, emitter_rate, *surface):
        layers, rows, _ = soil_head.shape
        run = make_kernel(
            n_grp, n_tile, layers, rows, soil_table.shape[1], emitter_cell.shape[-1]
        )
        return run(soil_head, soil_type, soil_table, emitter_cell, emitter_rate, *surface)

    cells = P(None, "grp", "tile")
    strip = P(("grp", "tile"), None)
    emitters = P("grp", "tile", None)
    return jax.shard_map(
        shards,
        mesh=mesh,
        in_specs=(cells, cells, P(), emitters, emitters, strip, strip, strip, strip, strip),
        out_specs=(cells, strip),
        check_vma=False,
    )
```

```python
import functools

import jax
import jax.numpy as jnp
from jax import lax
from jax.experimental import pallas as pl
from jax.experimental.pallas import tpu as pltpu
from jax.sharding import PartitionSpec as P

MESH = pl.DeviceIdType.MESH
STEPS = 2
PICARD = 2
ROUNDS = STEPS * PICARD
LANES = 128
STORAGE = 0.05
FILM_FLOOR = 0.04
BLEND = 0.05
LOG2E = 1.4426950408889634
OUTSIDE = 1e-30
PLANES = 8
WS, WD = 2, 3
H, SAT, SHP, CAP, EM = 0, 2, 3, 4, 5
SIDES = ((0, -1), (0, 1), (-1, 0), (1, 0), (1, 1), (1, -1), (-1, 1), (-1, -1))


def inverse(x):
    return pl.reciprocal(x, approx=True)


def face_of(a, b):
    return (a + a) * b * inverse(a + b)


def film_face(a, b):
    return (a + a) * b * inverse(a + b + BLEND)


def roll(x, shift):
    return pltpu.roll(x, shift % LANES, 1)


def make_kernel(n_grp, n_tile, layers, rows, n_types, n_emit):
    XI = rows // 8
    RP = XI + 16
    ZP = (PLANES + 2 * WS) * RP
    SP = (PLANES + 2 * WD) * RP
    nq = XI // 8
    top = layers - 1
    N = XI + 8
    yv = (WD * nq + 7) // 8

    def kernel(
        head_in, type_in, table, cell, rate, depth_in, elev_in, rough_in, pond_in, rain_in,
        head_out, depth_out,
        BIG, G1, K, FX, FY, FZ, RD, B, C, NAT, TYPE,
        A_SEND, A_RECV, ROUGH, POND, DN,
        SF, FILM, ETA, ETA2, GX, GY, SB, SRD,
        YS, YR, XS, XR, CS, CR, TYS, TYR, TXS, TXR, TCS, TCR,
        load_sem, a_send, a_recv, o_send, o_recv, out_sem,
        c_send, c_recv, t_send, t_recv,
    ):
        g = lax.axis_index("grp")
        t = lax.axis_index("tile")

        def inside(dg, dt):
            ok = jnp.bool_(True)
            if dg:
                ok = g + dg >= 0 if dg < 0 else g + dg < n_grp
            if dt:
                side = t + dt >= 0 if dt < 0 else t + dt < n_tile
                ok = jnp.logical_and(ok, side) if dg else side
            return ok

        has = [inside(dg, dt) for dg, dt in SIDES]
        came = [inside(-dg, -dt) for dg, dt in SIDES]
        target = [(g + dg, t + dt) for dg, dt in SIDES]

        loads = [
            pltpu.make_async_copy(rough_in, ROUGH, load_sem.at[0]),
            pltpu.make_async_copy(pond_in, POND, load_sem.at[1]),
            pltpu.make_async_copy(depth_in, A_SEND.at[0], load_sem.at[2]),
            pltpu.make_async_copy(elev_in, A_SEND.at[1], load_sem.at[3]),
            pltpu.make_async_copy(rain_in, A_SEND.at[3], load_sem.at[4]),
            pltpu.make_async_copy(type_in, TYPE, load_sem.at[5]),
            pltpu.make_async_copy(head_in, NAT, load_sem.at[6]),
        ]
        for copy in loads:
            copy.start()

        barrier = pltpu.get_barrier_semaphore()

        @pl.loop(1, n_tile)
        def _(d):
            pl.semaphore_signal(
                barrier, inc=1, device_id=(g, lax.rem(t + d, n_tile)), device_id_type=MESH
            )

        for side in range(2, 8):

            @pl.when(has[side])
            def _():
                pl.semaphore_signal(barrier, inc=1, device_id=target[side], device_id_type=MESH)

        lane = lax.broadcasted_iota(jnp.int32, (8, LANES), 1)
        xb = lax.bitwise_and(lane, 7)
        zero8 = jnp.zeros((8, LANES), jnp.float32)

        @pl.loop(0, ZP // 8)
        def _(r):
            for base in (0, (layers + 1) * ZP):
                at = pl.ds(pl.multiple_of(base + r * 8, 8), 8)
                BIG[H, at, :] = zero8
                BIG[H + 1, at, :] = zero8
                G1[at, :] = zero8
                K[at, :] = zero8
            FZ[pl.ds(pl.multiple_of(r * 8, 8), 8), :] = zero8

        for side in range(8):

            @pl.when(jnp.logical_not(came[side]))
            def _():
                for k in range(5 + ROUNDS - 1):
                    fill = zero8 + OUTSIDE if k == 1 else zero8
                    if side < 2:
                        for z in range(layers):
                            YR[side, k, z] = fill
                    elif side < 4:
                        for v in range(4):
                            XR[side - 2, k, v] = fill
                    else:
                        CR[side - 4, k] = fill
                for k in range(4 + ROUNDS - 1):
                    if side < 2:
                        for v in range(yv):
                            TYR[side, k, v] = zero8
                    elif side < 4:
                        TXR[side - 2, k] = zero8
                    else:
                        TCR[side - 4, k] = zero8

        def copies(bufs, k, count, send, recv):
            y_out, y_in, x_out, x_in, c_out, c_in = bufs
            at = pl.ds(k, count)
            out = []
            for side in range(8):
                if side < 2:
                    src, dst = y_out.at[at], y_in.at[side, at]
                elif side < 4:
                    src, dst = x_out.at[at], x_in.at[side - 2, at]
                else:
                    src, dst = c_out.at[side - 4, at], c_in.at[side - 4, at]
                out.append(
                    functools.partial(
                        pltpu.make_async_remote_copy,
                        src_ref=src,
                        dst_ref=dst,
                        send_sem=send.at[side],
                        recv_sem=recv.at[side],
                        device_id=target[side],
                        device_id_type=MESH,
                    )
                )
            return out

        soil_bufs = (YS, YR, XS, XR, CS, CR)
        surface_bufs = (TYS, TYR, TXS, TXR, TCS, TCR)

        def soil_copies(e):
            if isinstance(e, int) and e == 0:
                return copies(soil_bufs, 0, 5, c_send.at[0], c_recv.at[0])
            return copies(soil_bufs, 4 + e, 1, c_send.at[e], c_recv.at[e])

        def surface_copies(e):
            if isinstance(e, int) and e == 0:
                return copies(surface_bufs, 0, 4, t_send.at[0], t_recv.at[0])
            return copies(surface_bufs, 3 + e, 1, t_send.at[e], t_recv.at[e])

        def start(made, sides=(4, 5, 6, 7, 1, 0, 2, 3)):
            for side in sides:

                @pl.when(has[side])
                def _():
                    made[side]().start()

        def wait_recv(made, sides=range(8)):
            for side in sides:

                @pl.when(came[side])
                def _():
                    made[side]().wait_recv()

        def wait_send(made):
            for side in range(8):

                @pl.when(has[side])
                def _():
                    made[side]().wait_send()

        def fold(v):
            v = list(v)
            for k in (1, 2, 4):
                low = lax.bitwise_and(lane, k) == 0
                for a in range(8):
                    if a & k == 0:
                        p, q = v[a], v[a | k]
                        v[a] = jnp.where(low, p, roll(q, k))
                        v[a | k] = jnp.where(low, roll(p, -k), q)
            return v

        def zbase(z):
            return pl.multiple_of((z + 1) * ZP, 8)

        def soil_row(plane, xi):
            return (plane + WS) * RP + 8 + xi

        def film_row(plane, xi):
            return (plane + WD) * RP + 8 + xi

        def columns_out(R, row, width, jobs):
            spots = [(a, q) for a in range(1, width + 1) for q in range(nq)]
            read = []
            for base, put, values in jobs:
                for a, q in spots:
                    if values is None:
                        high = R[pl.ds(base + row(PLANES - a, 8 * q), 8), :]
                        low = R[pl.ds(base + row(a - 1, 8 * q), 8), :]
                    else:
                        high = values[PLANES - a][8 * q : 8 * q + 8]
                        low = values[a - 1][8 * q : 8 * q + 8]
                    read.append((high, low))
            moved = [(roll(high, 8), roll(low, -8)) for high, low in read]
            packs = []
            for n in range(len(jobs)):
                packed = zero8
                for i in range(len(spots)):
                    high, low = moved[n * len(spots) + i]
                    both = roll(jnp.where(lane >= LANES // 2, low, high), 16 * (i % 8) + 8)
                    packed = jnp.where(lax.shift_right_logical(lane, 4) == i % 8, both, packed)
                    if i % 8 == 7 or i == len(spots) - 1:
                        packs.append((n, i // 8, packed))
                        packed = zero8
            for n, (base, put, values) in enumerate(jobs):
                for i, (a, q) in enumerate(spots):
                    high, low = moved[n * len(spots) + i]
                    R[pl.ds(base + row(-a, 8 * q), 8), :] = high
                    R[pl.ds(base + row(PLANES - 1 + a, 8 * q), 8), :] = low
            for n, v, packed in packs:
                jobs[n][1](v, packed)

        def columns_in(R, row, width, jobs):
            spots = [(a, q) for a in range(1, width + 1) for q in range(nq)]
            todo = []
            for base, get in jobs:
                for i, (a, q) in enumerate(spots):
                    if i % 8 == 0:
                        from_right, from_left = get(i // 8)
                        met = jnp.where(lax.bitwise_and(lane, 15) < 8, from_right, from_left)
                    left = pl.ds(base + row(-a, 8 * q), 8)
                    right = pl.ds(base + row(PLANES - 1 + a, 8 * q), 8)
                    u = roll(met, -(16 * (i % 8) + 8))
                    todo.append((left, right, u, R[left, :], R[right, :]))
            for left, right, u, was_left, was_right in todo:
                R[left, :] = jnp.where(lane < 8, u, was_left)
                R[right, :] = jnp.where(lane >= LANES - 8, u, was_right)

        def rows_out(R, row, jobs, packs):
            read = []
            for base, b, slot, v in jobs:
                high = R[pl.ds(base + row(0, XI - b), 8, stride=RP), :]
                low = R[pl.ds(base + row(0, b - 1), 8, stride=RP), :]
                read.append((roll(high, 1), roll(low, -1)))
            for (base, b, slot, v), (high, low) in zip(jobs, read):
                both = roll(jnp.where(xb == 7, low, high), 2 * slot + 1)
                mine = lax.shift_right_logical(xb, 1) == slot
                packs[v] = jnp.where(mine, both, packs[v])
            for (base, b, slot, v), (high, low) in zip(jobs, read):
                R[pl.ds(base + row(0, -b), 8, stride=RP), :] = high
                R[pl.ds(base + row(0, XI - 1 + b), 8, stride=RP), :] = low

        def rows_meet(from_down, from_up):
            return jnp.where(lax.bitwise_and(lane, 1) == 1, roll(from_up, -8), roll(from_down, 8))

        def rows_in(R, row, jobs, met):
            todo = []
            for base, b, slot, v in jobs:
                up = pl.ds(base + row(0, -b), 8, stride=RP)
                down = pl.ds(base + row(0, XI - 1 + b), 8, stride=RP)
                todo.append((up, down, roll(met[v], -(2 * slot + 1)), R[up, :], R[down, :]))
            for up, down, u, was_up, was_down in todo:
                R[up, :] = jnp.where(xb == 0, u, was_up)
                R[down, :] = jnp.where(xb == 7, u, was_down)

        def corner_source(gather, side, a, b):
            plane = PLANES - a if side in (4, 6) else a - 1
            xi = XI - b if side in (4, 5) else b - 1
            return roll(gather(plane, xi), {4: 1, 5: 113, 6: 15, 7: 127}[side])

        def corner_value(gather, side, a, b, diagonal):
            ln = lane[: diagonal.shape[0]]
            x8 = xb[: diagonal.shape[0]]
            first = side in (4, 6)
            plane = -a if first else PLANES - 1 + a
            if side in (4, 5):
                inner = roll(gather(plane, XI - b), 1)
                other = gather(PLANES - a if first else a - 1, -b)
                near = x8 > 0
            else:
                inner = roll(gather(plane, b - 1), -1)
                other = gather(PLANES - a if first else a - 1, XI - 1 + b)
                near = x8 < 7
            other = roll(other, 8 if first else -8)
            known = ln >= 8 if first else ln < LANES - 8
            return jnp.where(near, inner, jnp.where(known, other, diagonal))

        def corner_place(side, a, b):
            return -a if side in (4, 6) else PLANES - 1 + a, -b if side in (4, 5) else XI - 1 + b

        def soil_put(k, z):
            def put(v, value):
                YS[k, z] = value

            return put

        def soil_jobs(width):
            return [
                ((z + 1) * ZP, b, z % 4, (b - 1) * 2 + z // 4)
                for z in range(layers)
                for b in range(1, width + 1)
            ]

        def soil_gather(R):
            def gather(plane, xi):
                return R[pl.ds(ZP + soil_row(plane, xi), layers, stride=ZP), :]

            return gather

        def soil_corners_out(f, k):
            for side in range(4, 8):
                CS[side - 4, k] = corner_source(soil_gather(BIG.at[f]), side, 1, 1)

        def soil_rows_out(f, k, width):
            packs = [zero8] * 4
            rows_out(BIG.at[f], soil_row, soil_jobs(width), packs)
            for v in range(4):
                XS[k, v] = packs[v]

        def soil_rows_in(f, k, width):
            met = [rows_meet(XR[0, k, v], XR[1, k, v]) for v in range(4)]
            rows_in(BIG.at[f], soil_row, soil_jobs(width), met)

        def soil_columns_in(f, k, width):
            @pl.loop(0, layers // 4)
            def _(h):
                columns_in(
                    BIG.at[f], soil_row, width,
                    [
                        (zbase(4 * h + n), lambda v, z=4 * h + n: (YR[0, k, z], YR[1, k, z]))
                        for n in range(4)
                    ],
                )

        def soil_corners_in(f, k):
            R = BIG.at[f]
            values = [
                corner_value(soil_gather(R), side, 1, 1, CR[side - 4, k]) for side in range(4, 8)
            ]
            for side in range(4, 8):
                plane, xi = corner_place(side, 1, 1)
                R[pl.ds(ZP + soil_row(plane, xi), layers, stride=ZP), :] = values[side - 4]

        corners = ((1, 1), (1, 2), (2, 1))

        def surface_out(f, k):
            R = SF.at[f]

            def put(v, value):
                TYS[k, v] = value

            columns_out(R, film_row, WD, [(0, put, None)])
            packs = [zero8]
            rows_out(R, film_row, [(0, b, b - 1, 0) for b in range(1, WD + 1)], packs)
            TXS[k] = packs[0]

            def gather(plane, xi):
                return R[pl.ds(film_row(plane, xi), 1), :]

            for side in range(4, 8):
                for n, (a, b) in enumerate(corners):
                    TCS[side - 4, k, pl.ds(n, 1), :] = corner_source(gather, side, a, b)

        def surface_in(f, k):
            R = SF.at[f]
            columns_in(R, film_row, WD, [(0, lambda v: (TYR[0, k, v], TYR[1, k, v]))])
            met = [rows_meet(TXR[0, k], TXR[1, k])]
            rows_in(R, film_row, [(0, b, b - 1, 0) for b in range(1, WD + 1)], met)

            def gather(plane, xi):
                return R[pl.ds(film_row(plane, xi), 1), :]

            for side in range(4, 8):
                for n, (a, b) in enumerate(corners):
                    value = corner_value(gather, side, a, b, TCR[side - 4, k, pl.ds(n, 1), :])
                    plane, xi = corner_place(side, a, b)
                    R[pl.ds(film_row(plane, xi), 1), :] = value

        @pl.loop(0, 4 + ROUNDS - 1)
        def _(k):
            for side in range(4):
                TCS[side, k] = zero8

        loads[5].wait()
        loads[6].wait()

        @pl.loop(0, layers)
        def _(z):
            base = (z + 1) * ZP
            for q in range(nq):
                kinds = fold(
                    [TYPE[z, pl.ds(i * XI + 8 * q, 8), :].astype(jnp.float32) for i in range(8)]
                )
                heads = fold([NAT[z, pl.ds(i * XI + 8 * q, 8), :] for i in range(8)])
                for plane in range(PLANES):
                    at = pl.ds(pl.multiple_of(base + soil_row(plane, 8 * q), 8), 8)
                    sat = shp = cap = zero8
                    for c in range(n_types):
                        same = kinds[plane] == float(c)
                        sat = jnp.where(same, table[0, c], sat)
                        shp = jnp.where(same, table[1, c] * LOG2E, shp)
                        cap = jnp.where(same, table[2, c], cap)
                    BIG[SAT, at, :] = sat
                    BIG[SHP, at, :] = shp
                    BIG[CAP, at, :] = cap
                    BIG[H, at, :] = heads[plane]

        ids = jnp.broadcast_to(cell[0], (LANES, n_emit))
        amount = jnp.broadcast_to(rate[0], (LANES, n_emit))
        column = lax.bitwise_and(ids, LANES - 1)
        line = lax.rem(lax.shift_right_logical(ids, 7), rows)
        layer = lax.div(lax.shift_right_logical(ids, 7), rows)
        wanted_lane = lax.bitwise_and(column, LANES - 8) + lax.div(line, XI)
        plane_row = lax.bitwise_and(column, 7) * XI + lax.rem(line, XI) + layer * rows
        here = wanted_lane == lax.broadcasted_iota(jnp.int32, (LANES, n_emit), 0)
        picked = jnp.where(here, amount, 0.0)
        part0 = picked.astype(jnp.bfloat16)
        rest = picked - part0.astype(jnp.float32)
        part1 = rest.astype(jnp.bfloat16)
        part2 = (rest - part1.astype(jnp.float32)).astype(jnp.bfloat16)

        @pl.loop(0, layers)
        def _(z):
            size = min(LANES, rows)
            for r in range(0, rows, size):
                wanted = lax.broadcasted_iota(jnp.int32, (size, n_emit), 0) + (z * rows + r)
                hot = jnp.where(plane_row[:size] == wanted, 1.0, 0.0).astype(jnp.bfloat16)
                total = jnp.zeros((size, LANES), jnp.float32)
                for part in (part2, part1, part0):
                    total = total + lax.dot_general(
                        hot, part, (((1,), (1,)), ((), ())), preferred_element_type=jnp.float32
                    )
                for s in range(0, size, XI):
                    plane = (r + s) // XI
                    at = pl.multiple_of((z + 1) * ZP + soil_row(plane, 0), 8)
                    BIG[EM, pl.ds(at, XI), :] = total[s : s + XI]

        for copy in loads[:5]:
            copy.wait()
        A_SEND[2] = ROUGH[...] * POND[...].astype(jnp.float32)
        own = pltpu.make_async_copy(
            A_SEND.at[:, :, pl.ds(pl.multiple_of(t * LANES, LANES), LANES)],
            A_RECV.at[:, pl.ds(pl.multiple_of(t * 8, 8), 8), :],
            a_recv,
        )
        own.start()

        beside = jnp.int32(0)
        for side in range(2, 8):
            beside = beside + came[side].astype(jnp.int32)
        pl.semaphore_wait(barrier, n_tile - 1 + beside)

        @pl.loop(1, n_tile)
        def _(d):
            peer = lax.rem(t + d, n_tile)
            pltpu.make_async_remote_copy(
                src_ref=A_SEND.at[:, :, pl.ds(pl.multiple_of(peer * LANES, LANES), LANES)],
                dst_ref=A_RECV.at[:, pl.ds(pl.multiple_of(t * 8, 8), 8), :],
                send_sem=a_send,
                recv_sem=a_recv,
                device_id=(g, peer),
                device_id_type=MESH,
            ).start()

        for first, last, width in ((0, 3, WS), (3, 5, 1)):

            @pl.loop(first, last)
            def _(k):
                field = jnp.where(k == 0, 0, k + 1)

                @pl.loop(0, layers // 2)
                def _(h):
                    columns_out(
                        BIG.at[field], soil_row, width,
                        [(zbase(2 * h + n), soil_put(k, 2 * h + n), None) for n in range(2)],
                    )

                soil_corners_out(field, k)
                soil_rows_out(field, k, width)

        start(soil_copies(0))

        D, ELEV, GAIN, RAIN = 0, 2, 3, 4

        @pl.loop(0, ROUNDS)
        def _(p):
            slot = lax.rem(p, 2)
            other = 1 - slot
            src = BIG.at[slot]
            dst = BIG.at[other]
            depth = SF.at[slot]

            def react(at, base_too):
                grow = jnp.exp2(BIG[SHP, at, :] * jnp.minimum(src[at, :], 0.0))
                K[at, :] = BIG[SAT, at, :] * grow
                if base_too:
                    store = BIG[CAP, at, :] * grow + STORAGE
                    C[at, :] = store
                    B[at, :] = store * BIG[H, at, :] + BIG[EM, at, :]

            @pl.loop(0, layers)
            def _(z):
                base = zbase(z)
                for plane in range(PLANES):
                    react(pl.ds(base + soil_row(plane, 0), XI), True)

            @pl.loop(0, layers)
            def _(z):
                base = zbase(z)
                for plane in range(PLANES):
                    at = pl.ds(base + soil_row(plane, 0), XI)
                    k = K[at, :]
                    FX[at, :] = face_of(k, K[pl.ds(base + soil_row(plane, 1), XI), :])
                    FZ[at, :] = face_of(k, K[pl.ds(base + ZP + soil_row(plane, 0), XI), :])
                    if plane < PLANES - 1:
                        FY[at, :] = face_of(k, K[pl.ds(base + soil_row(plane + 1, 0), XI), :])

            def first_at(base, plane, xi, size, stride=None):
                def spot(dz=0, dp=0, dx=0):
                    return pl.ds(base + dz * ZP + soil_row(plane + dp, xi + dx), size, stride=stride)

                at, before, left, down = spot(), spot(dx=-1), spot(dp=-1), spot(dz=-1)
                fx, fxm, fy, fym = FX[at, :], FX[before, :], FY[at, :], FY[left, :]
                above, below = FZ[at, :], FZ[down, :]
                scale = inverse(C[at, :] + fx + fxm + fy + fym + above + below)
                RD[at, :] = scale
                total = (
                    B[at, :]
                    + (above - below)
                    + fx * src[spot(dx=1), :]
                    + fxm * src[before, :]
                    + fy * src[spot(dp=1), :]
                    + fym * src[left, :]
                    + above * src[spot(dz=1), :]
                    + below * src[down, :]
                )
                G1[at, :] = total * scale

            def first_outer(base):
                for plane in (-1, 0, PLANES - 1, PLANES):
                    first_at(base, plane, -1, N)
                for xi in (-1, 0, XI - 1, XI):
                    first_at(base, 0, xi, 8, RP)

            @pl.loop(0, top)
            def _(z):
                for plane in range(1, PLANES - 1):
                    first_at(zbase(z), plane, 0, XI)

            @pl.when(p == 0)
            def _():
                pltpu.make_async_copy(A_RECV, A_RECV, a_recv).wait()

                @pl.loop(0, 4)
                def _(n):
                    field = jnp.where(n == 0, 0, n + 1)
                    for q in range(nq):
                        parts = fold([A_RECV[n, pl.ds(i * XI + 8 * q, 8), :] for i in range(8)])
                        for plane in range(PLANES):
                            SF[field, pl.ds(film_row(plane, 8 * q), 8), :] = parts[plane]

                @pl.loop(0, 4)
                def _(k):
                    surface_out(jnp.where(k == 0, 0, k + 1), k)

                start(surface_copies(0))
                wait_recv(soil_copies(0))

                for first, last, width in ((0, 3, WS), (3, 5, 1)):

                    @pl.loop(first, last)
                    def _(k):
                        field = jnp.where(k == 0, 0, k + 1)
                        soil_rows_in(field, k, width)
                        soil_columns_in(field, k, width)
                        soil_corners_in(field, k)

            @pl.when(p > 0)
            def _():
                wait_recv(soil_copies(p), (2, 3))
                soil_rows_in(slot, 4 + p, WS)
                wait_recv(soil_copies(p), (0, 1))
                soil_columns_in(slot, 4 + p, WS)
                wait_recv(soil_copies(p), (4, 5, 6, 7))
                soil_corners_in(slot, 4 + p)

            def line(base, plane, xi):
                return pl.ds(base + soil_row(plane, xi), 8, stride=RP)

            def outer_react(base):
                for plane in (-2, -1, PLANES, PLANES + 1):
                    react(pl.ds(base + soil_row(plane, -2), N), plane in (-1, PLANES))
                for xi in (-2, -1, XI, XI + 1):
                    react(line(base, 0, xi), xi in (-1, XI))

            last = p == ROUNDS - 1

            @pl.loop(jnp.where(last, top, 0), layers)
            def _(z):
                outer_react(zbase(z))

            def outer_faces(base):
                for plane in (-2, -1, PLANES - 1, PLANES):
                    at = pl.ds(base + soil_row(plane, -1), N)
                    k = K[at, :]
                    FY[at, :] = face_of(k, K[pl.ds(base + soil_row(plane + 1, -1), N), :])
                    if plane in (-1, PLANES):
                        FZ[at, :] = face_of(k, K[pl.ds(base + ZP + soil_row(plane, -1), N), :])
                        before = pl.ds(base + soil_row(plane, -2), N)
                        FX[before, :] = face_of(K[before, :], k)
                for xi in (-2, -1, XI - 1, XI):
                    at = line(base, 0, xi)
                    k = K[at, :]
                    FX[at, :] = face_of(k, K[line(base, 0, xi + 1), :])
                    if xi in (-1, XI):
                        FZ[at, :] = face_of(k, K[line(base + ZP, 0, xi), :])
                        FY[at, :] = face_of(k, K[line(base, 1, xi), :])

            @pl.loop(0, jnp.where(p < ROUNDS - 1, layers, 0))
            def _(z):
                outer_faces(zbase(z))

            early = jnp.where(p < ROUNDS - 1, top, 0)

            @pl.loop(0, early)
            def _(z):
                first_outer(zbase(z))

            @pl.when(p == 0)
            def _():
                wait_recv(surface_copies(0))

                @pl.loop(0, 4)
                def _(k):
                    surface_in(jnp.where(k == 0, 0, k + 1), k)

            @pl.when(p > 0)
            def _():
                wait_recv(surface_copies(p))
                surface_in(slot, 3 + p)

            for plane in range(-3, PLANES + 3):
                at = pl.ds(film_row(plane, -3), N)
                d = depth[at, :]
                square = d * d + FILM_FLOOR
                FILM[at, :] = SF[GAIN, at, :] * (square * lax.rsqrt(square))
                ETA[at, :] = SF[ELEV, at, :] + d
            for plane in range(-3, PLANES + 2):
                at = pl.ds(film_row(plane, -3), N)
                film = FILM[at, :]
                GX[at, :] = film_face(film, FILM[pl.ds(film_row(plane, -2), N), :])
                GY[at, :] = film_face(film, FILM[pl.ds(film_row(plane + 1, -3), N), :])

            def film_sum(source, plane, first):
                at = pl.ds(film_row(plane, first), N)
                after = pl.ds(film_row(plane, first + 1), N)
                before = pl.ds(film_row(plane, first - 1), N)
                right = pl.ds(film_row(plane + 1, first), N)
                left = pl.ds(film_row(plane - 1, first), N)
                return (
                    SB[at, :]
                    + GX[at, :] * source[after, :]
                    + GX[before, :] * source[before, :]
                    + GY[at, :] * source[right, :]
                    + GY[left, :] * source[left, :]
                ) * SRD[at, :]

            high = (top + 1) * ZP
            for plane in range(-2, PLANES + 2):
                at = pl.ds(film_row(plane, -2), N)
                soil_at = pl.ds(high + soil_row(plane, -2), N)
                faces = (
                    GX[at, :]
                    + GX[pl.ds(film_row(plane, -3), N), :]
                    + GY[at, :]
                    + GY[pl.ds(film_row(plane - 1, -2), N), :]
                )
                cond = K[soil_at, :]
                start_level = SF[D, at, :] + SF[RAIN, at, :] + cond * src[soil_at, :]
                SB[at, :] = start_level - faces * SF[ELEV, at, :]
                SRD[at, :] = inverse(1.0 + cond + faces)
                ETA2[at, :] = film_sum(ETA, plane, -2) + SF[ELEV, at, :]
            for plane in range(-1, PLANES + 1):
                at = pl.ds(film_row(plane, -1), N)
                soil_at = pl.ds(high + soil_row(plane, -1), N)
                d = film_sum(ETA2, plane, -1)
                SF[other, at, :] = d
                B[soil_at, :] = B[soil_at, :] + K[soil_at, :] * (d - src[soil_at, :])

            @pl.when(p < ROUNDS - 1)
            def _():
                surface_out(other, 4 + p)
                start(surface_copies(p + 1))

            @pl.when(p == ROUNDS - 1)
            def _():
                for q in range(nq):
                    parts = fold([SF[D, pl.ds(film_row(i, 8 * q), 8), :] for i in range(8)])
                    for i in range(8):
                        DN[pl.ds(i * XI + 8 * q, 8), :] = parts[i]
                pltpu.make_async_copy(
                    DN.at[pl.ds(pl.multiple_of(t * 8, 8), 8), :],
                    depth_out.at[:, pl.ds(pl.multiple_of(t * LANES, LANES), LANES)],
                    o_recv,
                ).start()

                @pl.loop(1, n_tile)
                def _(d):
                    peer = lax.rem(t + d, n_tile)
                    pltpu.make_async_remote_copy(
                        src_ref=DN.at[pl.ds(pl.multiple_of(peer * 8, 8), 8), :],
                        dst_ref=depth_out.at[:, pl.ds(pl.multiple_of(t * LANES, LANES), LANES)],
                        send_sem=o_send,
                        recv_sem=o_recv,
                        device_id=(g, peer),
                        device_id_type=MESH,
                    ).start()

            def soil_sum(source, base, plane, first, size, at, value, below, above):
                after = pl.ds(base + soil_row(plane, first + 1), size)
                before = pl.ds(base + soil_row(plane, first - 1), size)
                right = pl.ds(base + soil_row(plane + 1, first), size)
                left = pl.ds(base + soil_row(plane - 1, first), size)
                return (
                    value
                    + FX[at, :] * source[after, :]
                    + FX[before, :] * source[before, :]
                    + FY[at, :] * source[right, :]
                    + FY[left, :] * source[left, :]
                    + above * source[pl.ds(base + ZP + soil_row(plane, first), size), :]
                    + below * source[pl.ds(base - ZP + soil_row(plane, first), size), :]
                )

            @pl.loop(0, jnp.where(last, top, 0))
            def _(z):
                outer_react(zbase(z))

            @pl.loop(jnp.where(p < ROUNDS - 1, layers, 0), layers)
            def _(z):
                outer_faces(zbase(z))

            @pl.loop(early, top)
            def _(z):
                first_outer(zbase(z))

            for plane in range(-1, PLANES + 1):
                first_at(high, plane, -1, N)

            def second_sweep(base):
                values = []
                for plane in range(PLANES):
                    at = pl.ds(base + soil_row(plane, 0), XI)
                    below = FZ[pl.ds(base - ZP + soil_row(plane, 0), XI), :]
                    total = soil_sum(
                        G1, base, plane, 0, XI, at, B[at, :] + (FZ[at, :] - below), below, FZ[at, :]
                    )
                    values.append(total * RD[at, :])
                    dst[at, :] = values[-1]
                return values

            @pl.when(p < ROUNDS - 1)
            def _():
                @pl.loop(0, layers)
                def _(z):
                    base = zbase(z)
                    values = second_sweep(base)
                    columns_out(dst, soil_row, WS, [(base, soil_put(5 + p, z), values)])

                soil_corners_out(other, 5 + p)
                start(soil_copies(p + 1), (4, 5, 6, 7, 1, 0))
                soil_rows_out(other, 5 + p, WS)
                start(soil_copies(p + 1), (2, 3))

            @pl.when(p == ROUNDS - 1)
            def _():
                @pl.loop(0, layers)
                def _(z):
                    base = zbase(z)
                    values = second_sweep(base)
                    for q in range(nq):
                        parts = fold([values[i][8 * q : 8 * q + 8] for i in range(8)])
                        for i in range(8):
                            NAT[z, pl.ds(i * XI + 8 * q, 8), :] = parts[i]
                    pltpu.make_async_copy(NAT.at[z], head_out.at[z], out_sem).start()

        wait_send(soil_copies(0))
        wait_send(surface_copies(0))

        @pl.loop(1, ROUNDS)
        def _(e):
            wait_send(soil_copies(e))
            wait_send(surface_copies(e))

        sent = A_SEND.at[:, :, pl.ds(0, (n_tile - 1) * LANES)]
        pltpu.make_async_copy(sent, sent, a_send).wait()
        gone = DN.at[pl.ds(0, (n_tile - 1) * 8), :]
        pltpu.make_async_copy(gone, gone, o_send).wait()
        pltpu.make_async_copy(depth_out, depth_out, o_recv).wait()
        pltpu.make_async_copy(NAT, head_out, out_sem).wait()

    f32 = jnp.float32

    def vmem(*shape, dtype=f32):
        return pltpu.VMEM(shape, dtype)

    wide = n_tile * LANES
    dma = pltpu.SemaphoreType.DMA
    tall = (layers + 2) * ZP
    ks, kd = 5 + ROUNDS - 1, 4 + ROUNDS - 1
    scratch = [
        vmem(6, tall, LANES),
        vmem(tall, LANES),
        vmem(tall, LANES),
        vmem(tall, LANES),
        vmem(tall, LANES),
        vmem(tall, LANES),
        vmem(tall, LANES),
        vmem(tall, LANES),
        vmem(tall, LANES),
        vmem(layers, rows, LANES),
        vmem(layers, rows, LANES, dtype=jnp.int32),
        vmem(4, 8, wide),
        vmem(4, rows, LANES),
        vmem(8, wide),
        vmem(8, wide, dtype=jnp.int32),
        vmem(rows, LANES),
        vmem(5, SP, LANES),
        vmem(SP, LANES),
        vmem(SP, LANES),
        vmem(SP, LANES),
        vmem(SP, LANES),
        vmem(SP, LANES),
        vmem(SP, LANES),
        vmem(SP, LANES),
        vmem(ks, layers, 8, LANES),
        vmem(2, ks, layers, 8, LANES),
        vmem(ks, 4, 8, LANES),
        vmem(2, ks, 4, 8, LANES),
        vmem(4, ks, 8, LANES),
        vmem(4, ks, 8, LANES),
        vmem(kd, yv, 8, LANES),
        vmem(2, kd, yv, 8, LANES),
        vmem(kd, 8, LANES),
        vmem(2, kd, 8, LANES),
        vmem(4, kd, 8, LANES),
        vmem(4, kd, 8, LANES),
        dma((7,)), dma(()), dma(()), dma(()), dma(()), dma(()),
        dma((ROUNDS, 8)), dma((ROUNDS, 8)), dma((ROUNDS, 8)), dma((ROUNDS, 8)),
    ]
    anywhere = pl.BlockSpec(memory_space=pl.ANY)
    in_vmem = pl.BlockSpec(memory_space=pltpu.VMEM)
    return pl.pallas_call(
        kernel,
        out_shape=(
            jax.ShapeDtypeStruct((layers, rows, LANES), f32),
            jax.ShapeDtypeStruct((8, wide), f32),
        ),
        in_specs=[
            anywhere, anywhere, pl.BlockSpec(memory_space=pltpu.SMEM), in_vmem, in_vmem,
            anywhere, anywhere, anywhere, anywhere, anywhere,
        ],
        out_specs=(anywhere, anywhere),
        scratch_shapes=scratch,
        compiler_params=pltpu.CompilerParams(
            collective_id=0, has_side_effects=True, vmem_limit_bytes=60 * 1024 * 1024
        ),
    )


def solution(mesh):
    n_grp, n_tile = mesh.shape["grp"], mesh.shape["tile"]

    def shards(soil_head, soil_type, soil_table, emitter_cell, emitter_rate, *surface):
        layers, rows, _ = soil_head.shape
        run = make_kernel(
            n_grp, n_tile, layers, rows, soil_table.shape[1], emitter_cell.shape[-1]
        )
        return run(soil_head, soil_type, soil_table, emitter_cell, emitter_rate, *surface)

    cells = P(None, "grp", "tile")
    strip = P(("grp", "tile"), None)
    emitters = P("grp", "tile", None)
    return jax.shard_map(
        shards,
        mesh=mesh,
        in_specs=(cells, cells, P(), emitters, emitters, strip, strip, strip, strip, strip),
        out_specs=(cells, strip),
        check_vma=False,
    )
```
